256 devices in a mesh: frame: 8 (over y_hi, x), tile: 32 (over z, y_lo, core).
Axes of the slice: x: 4, y: 4 (y_hi: 2, y_lo: 2; y = y_hi * 2 + y_lo), z: 8, core: 2. Of those that a mesh axis runs over, the one named last changes fastest.
Arguments:
- query_s: bfloat16 [16, 2048, 2048], P('frame', 'tile'), may hold values from -6 to 6
- key_s: bfloat16 [16, 2048, 2048], P('frame', 'tile'), may hold values from -6 to 6
- value_s: bfloat16 [16, 2048, 2048], P('frame', 'tile'), may hold values from -6 to 6
- grad_out_s: bfloat16 [16, 2048, 2048], P('frame', 'tile'), may hold values from -6 to 6
- query_t: bfloat16 [16, 2048, 2048], P('frame', 'tile'), may hold values from -6 to 6
- key_t: bfloat16 [16, 2048, 2048], P('frame', 'tile'), may hold values from -6 to 6
- value_t: bfloat16 [16, 2048, 2048], P('frame', 'tile'), may hold values from -6 to 6
- grad_out_t: bfloat16 [16, 2048, 2048], P('frame', 'tile'), may hold values from -6 to 6
- gains: float32 [4, 128], replicated, may hold values from 0.1 to 1.9
Outputs:
- out_s: bfloat16 [16, 2048, 2048], P('frame', 'tile')
- dquery_s: bfloat16 [16, 2048, 2048], P('frame', 'tile')
- dkey_s: bfloat16 [16, 2048, 2048], P('frame', 'tile')
- dvalue_s: bfloat16 [16, 2048, 2048], P('frame', 'tile')
- out_t: bfloat16 [16, 2048, 2048], P('frame', 'tile')
- dquery_t: bfloat16 [16, 2048, 2048], P('frame', 'tile')
- dkey_t: bfloat16 [16, 2048, 2048], P('frame', 'tile')
- dvalue_t: bfloat16 [16, 2048, 2048], P('frame', 'tile')
- gain_grads: float32 [4, 128], replicated
The draws below stay inside these ranges and needn't reach their ends.
All inputs are finite; a program needn't handle non-finite values.
Results may differ from the reference program's by a relative error of at most 0.014.
Values may be sent and summed in bfloat16 or wider, within the bound.
No kernel may reach another device: no remote copies, remote signals or barrier semaphores. Data moves between devices by JAX's collectives and lax.ppermute only.
A program may use at most 128 MiB of HBM per device.

```python
import jax
import jax.numpy as jnp
from jax import lax

HEADS = 16
HEAD_DIM = 128
TOK_FRAME = 2048
INNER = 2048
FRAMES = 16


def block_scale(stream_key, extent, pieces, low, high):
    level, own = 1.0, jax.random.fold_in(stream_key, 6)
    for axis_at, parts in pieces:
        draws = jnp.exp(jax.random.uniform(jax.random.fold_in(own, axis_at), (parts,), jnp.float32, low / len(pieces), high / len(pieces)))
        level = level * jnp.repeat(draws, extent[axis_at] // parts).reshape([-1 if axis == axis_at else 1 for axis in range(len(extent))])
    return level


def gaussian(rng, dims, deviation, reach, shards=(), dtype=jnp.bfloat16):
    entries = jax.random.normal(rng, dims, jnp.float32) * deviation
    if len(shards) > 0:
        entries = block_scale(rng, dims, shards, -0.22, 0.18) * entries
    return jnp.clip(entries, min=-reach, max=reach).astype(dtype)


def setup_inputs(seed: int = 0) -> dict:
    splits = jax.random.split(jax.random.key(seed), 10)
    return {
        "query_s": gaussian(splits[0], (FRAMES, TOK_FRAME, INNER), 1.0, 6.0, ((0, 8), (1, 32))),
        "key_s": gaussian(splits[1], (FRAMES, TOK_FRAME, INNER), 1.0, 6.0, ((0, 8), (1, 32))),
        "value_s": gaussian(splits[2], (FRAMES, TOK_FRAME, INNER), 1.0, 6.0, ((0, 8), (1, 32))),
        "grad_out_s": gaussian(splits[3], (FRAMES, TOK_FRAME, INNER), 1.0, 6.0, ((0, 8), (1, 32))),
        "query_t": gaussian(splits[4], (FRAMES, TOK_FRAME, INNER), 1.0, 6.0, ((0, 8), (1, 32))),
        "key_t": gaussian(splits[5], (FRAMES, TOK_FRAME, INNER), 1.0, 6.0, ((0, 8), (1, 32))),
        "value_t": gaussian(splits[6], (FRAMES, TOK_FRAME, INNER), 1.0, 6.0, ((0, 8), (1, 32))),
        "grad_out_t": gaussian(splits[7], (FRAMES, TOK_FRAME, INNER), 1.0, 6.0, ((0, 8), (1, 32))),
        "gains": jnp.clip(1.0 + 0.18 * jax.random.normal(splits[8], (4, HEAD_DIM), jnp.float32), 0.1, 1.9),
    }


EPS = 1e-06

def normalize(x, gain):
    xf = x.astype(jnp.float32)
    inverse = lax.rsqrt(lax.optimization_barrier(jnp.mean(xf * xf, axis=-1, keepdims=True)) + EPS)
    unit = xf * inverse
    return ((unit * gain).astype(jnp.bfloat16), unit, inverse)

def normalize_back(grad_hat, unit, inverse, gain):
    scaled = grad_hat * gain
    dgain = lax.optimization_barrier(jnp.sum((grad_hat * unit).reshape(-1, unit.shape[-1]), axis=0))
    dx = inverse * (scaled - unit * lax.optimization_barrier(jnp.mean(scaled * unit, axis=-1, keepdims=True)))
    return (dx.astype(jnp.bfloat16), dgain)

def attend(qh, kh, values, dout):
    f32 = jnp.float32
    scale = qh.shape[-1] ** (-0.5)
    scores = jnp.einsum('ble,bse->bls', qh.astype(f32), kh.astype(f32)) * scale
    expo = jnp.exp(scores)
    probs = expo / lax.optimization_barrier(jnp.sum(expo, axis=-1, keepdims=True))
    probs_b = probs.astype(jnp.bfloat16)
    out32 = jnp.einsum('bls,bse->ble', probs_b.astype(f32), values.astype(f32))
    dprob = jnp.einsum('ble,bse->bls', dout.astype(f32), values.astype(f32))
    delta = lax.optimization_barrier(jnp.sum(dout.astype(f32) * out32, axis=-1, keepdims=True))
    dscore = (probs * (dprob - delta)).astype(jnp.bfloat16)
    dqh = jnp.einsum('bls,bse->ble', dscore.astype(f32), kh.astype(f32)) * scale
    dkh = jnp.einsum('bls,ble->bse', dscore.astype(f32), qh.astype(f32)) * scale
    dval = jnp.einsum('bls,ble->bse', probs_b.astype(f32), dout.astype(f32))
    return (out32.astype(jnp.bfloat16), dqh, dkh, dval)

def layer(query, key, value, dout, gain_q, gain_k):
    qh, q_unit, q_inv = normalize(query, gain_q)
    kh, k_unit, k_inv = normalize(key, gain_k)
    out, dqh, dkh, dval = attend(qh, kh, value, dout)
    dquery, grad_q = normalize_back(dqh, q_unit, q_inv, gain_q)
    dkey, grad_k = normalize_back(dkh, k_unit, k_inv, gain_k)
    return (out, dquery, dkey, dval.astype(jnp.bfloat16), grad_q, grad_k)

def reference(query_s, key_s, value_s, grad_out_s, query_t, key_t, value_t, grad_out_t, gains):

    def spatial_frame(arrays):
        heads = [a.reshape(TOK_FRAME, HEADS, HEAD_DIM).transpose(1, 0, 2) for a in arrays]
        res = layer(heads[0], heads[1], heads[2], heads[3], gains[0], gains[1])
        back = tuple((r.transpose(1, 0, 2).reshape(TOK_FRAME, INNER) for r in res[:4]))
        return back + (res[4], res[5])
    spatial = lax.map(spatial_frame, (query_s, key_s, value_s, grad_out_s))
    grad_qs = lax.optimization_barrier(jnp.sum(spatial[4], axis=0))
    grad_ks = lax.optimization_barrier(jnp.sum(spatial[5], axis=0))

    def by_position(x):
        return x.reshape(FRAMES, TOK_FRAME, HEADS, HEAD_DIM).transpose(1, 2, 0, 3).reshape(TOK_FRAME * HEADS, FRAMES, HEAD_DIM)

    def by_frame(x):
        return x.reshape(TOK_FRAME, HEADS, FRAMES, HEAD_DIM).transpose(2, 0, 1, 3).reshape(FRAMES, TOK_FRAME, INNER)
    res = layer(by_position(query_t), by_position(key_t), by_position(value_t), by_position(grad_out_t), gains[2], gains[3])
    temporal = [by_frame(r) for r in res[:4]]
    gain_grads = jnp.stack([grad_qs, grad_ks, res[4], res[5]])
    return (spatial[0], spatial[1], spatial[2], spatial[3], temporal[0], temporal[1], temporal[2], temporal[3], gain_grads)
```

```python
import functools

import jax
import jax.numpy as jnp
from jax import lax
from jax.experimental import pallas as pl
from jax.experimental.pallas import tpu as pltpu
from jax.sharding import PartitionSpec as P

HEADS = 16
HEAD_DIM = 128
EPS = 1e-06
SCALE = HEAD_DIM**-0.5
LOG2E = 1.4426950408889634
BF16 = jnp.bfloat16
F32 = jnp.float32
SEQ = 2048
BLOCK = 256
ONES = 16
STEPS = ((0, 0), (0, 1), (0, 3), (1, 0), (1, 1), (1, 3), (0, 2), (1, 2))


def dot(a, b, ca, cb):
    return lax.dot_general(a, b, (((ca,), (cb,)), ((), ())), preferred_element_type=F32)


def params(mib):
    return pltpu.CompilerParams(vmem_limit_bytes=mib << 20)


def cost(flops, nbytes, trans=0):
    return pl.CostEstimate(flops=flops, bytes_accessed=nbytes, transcendentals=trans)


def inverse_rms(xf):
    return lax.rsqrt(jnp.mean(xf * xf, axis=-1, keepdims=True) + EPS)


def norm_back(grad_hat, x, gain):
    xf = x.astype(F32)
    inverse = inverse_rms(xf)
    unit = xf * inverse
    scaled = grad_hat * gain
    dgain = jnp.sum(grad_hat * unit, axis=0, keepdims=True)
    dx = inverse * (scaled - unit * jnp.mean(scaled * unit, axis=-1, keepdims=True))
    return dx.astype(BF16), dgain


def pack_s_kernel(q_ref, k_ref, v_ref, d_ref, o_ref):
    heads = o_ref.shape[1]
    for a, ref in enumerate((q_ref, k_ref, v_ref, d_ref)):
        for f in range(2):
            for h in range(heads):
                o_ref[f, h, a] = ref[f, :, h * HEAD_DIM : (h + 1) * HEAD_DIM]


def pack_s(arrays):
    frames, places, width = arrays[0].shape
    group = 4
    out = pl.pallas_call(
        pack_s_kernel,
        out_shape=jax.ShapeDtypeStruct((frames, HEADS, 4, places, HEAD_DIM), BF16),
        grid=(HEADS // group,),
        in_specs=[pl.BlockSpec((frames, places, group * HEAD_DIM), lambda i: (0, 0, i))] * 4,
        out_specs=pl.BlockSpec((frames, group, 4, places, HEAD_DIM), lambda i: (0, i, 0, 0, 0)),
        compiler_params=params(16),
        cost_estimate=cost(0, 4 << 20),
        name="pack_spatial",
    )(*arrays)
    return out.reshape(frames * HEADS, 4, places, HEAD_DIM)


def unpack_s_kernel(x_ref, *out_refs):
    heads = x_ref.shape[1]
    for a, ref in enumerate(out_refs):
        for f in range(2):
            for h in range(heads):
                ref[f, :, h * HEAD_DIM : (h + 1) * HEAD_DIM] = x_ref[f, h, a]


def unpack_s(x, frames):
    places = x.shape[2]
    group = 4
    return pl.pallas_call(
        unpack_s_kernel,
        out_shape=[jax.ShapeDtypeStruct((frames, places, HEADS * HEAD_DIM), BF16)] * 4,
        grid=(HEADS // group,),
        in_specs=[pl.BlockSpec((frames, group, 4, places, HEAD_DIM), lambda i: (0, i, 0, 0, 0))],
        out_specs=[pl.BlockSpec((frames, places, group * HEAD_DIM), lambda i: (0, 0, i))] * 4,
        compiler_params=params(16),
        cost_estimate=cost(0, 4 << 20),
        name="unpack_spatial",
    )(x.reshape(frames, HEADS, 4, places, HEAD_DIM))


def lanes_of(at_ref, j, width):
    return pl.ds(pl.multiple_of(at_ref[j] * width, width), width)


def pack_t_kernel(at_ref, q_ref, k_ref, v_ref, d_ref, *out_refs):
    width = out_refs[0].shape[-1]
    for j, out in enumerate(out_refs):
        lanes = lanes_of(at_ref, j, width)
        for a, ref in enumerate((q_ref, k_ref, v_ref, d_ref)):
            out[a] = ref[:, :, lanes]


def pack_t(at, arrays):
    frames, places, width = arrays[0].shape
    part = width // len(STEPS)
    return pl.pallas_call(
        pack_t_kernel,
        out_shape=[jax.ShapeDtypeStruct((4, frames, places, part), BF16)] * len(STEPS),
        in_specs=[pl.BlockSpec(memory_space=pltpu.SMEM)] + [pl.BlockSpec(memory_space=pltpu.VMEM)] * 4,
        out_specs=[pl.BlockSpec(memory_space=pltpu.VMEM)] * len(STEPS),
        compiler_params=params(16),
        cost_estimate=cost(0, 4 << 20),
        name="pack_temporal",
    )(at, *arrays)


def unpack_t_kernel(at_ref, *refs):
    parts, outs = refs[: len(STEPS)], refs[len(STEPS) :]
    width = parts[0].shape[-1]
    for j, part in enumerate(parts):
        lanes = lanes_of(at_ref, j, width)
        for a, out in enumerate(outs):
            out[:, :, lanes] = part[a]


def unpack_t(at, parts):
    _, frames, places, part = parts[0].shape
    return pl.pallas_call(
        unpack_t_kernel,
        out_shape=[jax.ShapeDtypeStruct((frames, places, part * len(STEPS)), BF16)] * 4,
        in_specs=[pl.BlockSpec(memory_space=pltpu.SMEM)]
        + [pl.BlockSpec(memory_space=pltpu.VMEM)] * len(STEPS),
        out_specs=[pl.BlockSpec(memory_space=pltpu.VMEM)] * 4,
        compiler_params=params(16),
        cost_estimate=cost(0, 4 << 20),
        name="unpack_temporal",
    )(at, *parts)


def temporal_kernel(gains_ref, *refs):
    count = len(STEPS)
    ins, outs, dgain_ref = refs[:count], refs[count : 2 * count], refs[2 * count]
    _, frames, places, width = ins[0].shape
    rows = count * frames * 16
    gain_q, gain_k = gains_ref[2:3, :], gains_ref[3:4, :]
    row = lax.broadcasted_iota(jnp.int32, (rows, rows), 0)
    column = lax.broadcasted_iota(jnp.int32, (rows, rows), 1)
    same = (row % 16) == (column % 16)
    dgain_ref[...] = jnp.zeros_like(dgain_ref)

    def step(block, _):
        at = pl.ds(pl.multiple_of(block * 16, 16), 16)
        for h in range(width // HEAD_DIM):
            lanes = slice(h * HEAD_DIM, (h + 1) * HEAD_DIM)

            def take(a):
                return jnp.concatenate([ref[a, f, at, lanes] for ref in ins for f in range(frames)], axis=0)

            query, key, value, dout = take(0), take(1), take(2), take(3)
            qf, kf = query.astype(F32), key.astype(F32)
            qh = (qf * inverse_rms(qf) * gain_q).astype(BF16)
            kh = (kf * inverse_rms(kf) * gain_k).astype(BF16)
            expo = jnp.where(same, jnp.exp(dot(qh, kh, 1, 1) * SCALE), 0.0)
            probs = expo / jnp.sum(expo, axis=-1, keepdims=True)
            probs_b = probs.astype(BF16)
            out = dot(probs_b, value, 1, 0)
            dprob = dot(dout, value, 1, 1)
            delta = jnp.sum(dout.astype(F32) * out, axis=-1, keepdims=True)
            dscore = (probs * (dprob - delta)).astype(BF16)
            dqh = dot(dscore, kh, 1, 0) * SCALE
            dkh = dot(dscore, qh, 0, 0) * SCALE
            dvalue = dot(probs_b, dout, 0, 0)
            dquery, dgain_q = norm_back(dqh, query, gain_q)
            dkey, dgain_k = norm_back(dkh, key, gain_k)
            dgain_ref[0:1, :] += dgain_q
            dgain_ref[1:2, :] += dgain_k
            for a, res in enumerate((out.astype(BF16), dquery, dkey, dvalue.astype(BF16))):
                for j, ref in enumerate(outs):
                    for f in range(frames):
                        first = (j * frames + f) * 16
                        ref[a, f, at, lanes] = res[first : first + 16]
        return 0

    lax.fori_loop(0, places // 16, step, 0)


def temporal(gains, parts):
    whole = pl.BlockSpec(memory_space=pltpu.VMEM)
    res = pl.pallas_call(
        temporal_kernel,
        out_shape=[jax.ShapeDtypeStruct(p.shape, BF16) for p in parts] + [jax.ShapeDtypeStruct((2, HEAD_DIM), F32)],
        in_specs=[whole] * (1 + len(parts)),
        out_specs=[whole] * (1 + len(parts)),
        compiler_params=params(24),
        cost_estimate=cost(8 * 6 * 2 * 256 * 256 * 128, 4 << 20, 8 * 65536),
        name="temporal_attention",
    )(gains, *parts)
    return res[:-1], res[-1]


def spatial_kernel(gains_ref, x_ref, out_ref, dgain_ref, qh, kh, kh_t, v_t, expo, dscore, out_t, dp_t, dp_n, dq_t):
    tiles, _, places, depth = x_ref.shape
    seq = tiles * places
    per = BLOCK // places
    gain_q, gain_k = gains_ref[0:1, :], gains_ref[1:2, :]

    def rows_of(b):
        return pl.ds(pl.multiple_of(b * BLOCK, BLOCK), BLOCK)

    def read(a, b):
        return x_ref[pl.ds(b * per, per), a].reshape(BLOCK, depth)

    def write(a, b, value):
        out_ref[pl.ds(b * per, per), a] = value.astype(BF16).reshape(per, places, depth)

    def prepare(b, _):
        rows = rows_of(b)
        qf = read(0, b).astype(F32)
        qh[rows, :] = (qf * inverse_rms(qf) * gain_q).astype(BF16)
        kf = read(1, b).astype(F32)
        k_hat = (kf * inverse_rms(kf) * gain_k).astype(BF16)
        kh[rows, :] = k_hat
        kh_t[:, rows] = k_hat.T
        v_t[0:depth, rows] = read(2, b).T
        v_t[depth:, rows] = jnp.ones((ONES, BLOCK), BF16)
        return 0

    lax.fori_loop(0, seq // BLOCK, prepare, 0)

    def forward(b, _):
        rows = rows_of(b)
        q_b = qh[rows, :]
        for c in range(seq // BLOCK):
            keys = slice(c * BLOCK, (c + 1) * BLOCK)
            scores = dot(kh[keys, :], q_b, 1, 1)
            expo[keys, rows] = jnp.exp2(scores * (SCALE * LOG2E)).astype(BF16)
        out_t[...] = dot(v_t[...], expo[:, rows], 1, 0)
        inverse = 1.0 / out_t[depth : depth + 1, :]
        o_t = out_t[0:depth, :] * inverse
        write(0, b, o_t.astype(BF16).T)
        d_t = (read(3, b).T.astype(F32) * inverse).astype(BF16)
        delta = jnp.sum(d_t.astype(F32) * o_t, axis=0, keepdims=True)
        dp_t[:, rows] = d_t
        dp_n[rows, :] = d_t.T
        for c in range(seq // BLOCK):
            keys = slice(c * BLOCK, (c + 1) * BLOCK)
            value = x_ref[c * per : (c + 1) * per, 2].reshape(BLOCK, depth)
            grad = dot(value, d_t, 1, 0)
            dscore[keys, rows] = (expo[keys, rows].astype(F32) * (grad - delta)).astype(BF16)
        dq_t[...] = dot(kh_t[...], dscore[:, rows], 1, 0) * SCALE
        dquery, dgain = norm_back(dq_t[...].T, read(0, b), gain_q)
        write(1, b, dquery)
        dgain_ref[0:1, :] += dgain
        return 0

    dgain_ref[...] = jnp.zeros_like(dgain_ref)
    lax.fori_loop(0, seq // BLOCK, forward, 0)

    def backward(b, _):
        rows = rows_of(b)
        dkh = dot(dscore[rows, :], qh[...], 1, 0) * SCALE
        dkey, dgain = norm_back(dkh, read(1, b), gain_k)
        write(2, b, dkey)
        dgain_ref[1:2, :] += dgain
        write(3, b, dot(expo[rows, :], dp_n[...], 1, 0))
        return 0

    lax.fori_loop(0, seq // BLOCK, backward, 0)


def spatial(gains, x):
    tiles, _, places, depth = x.shape
    seq = tiles * places
    whole = pl.BlockSpec(memory_space=pltpu.VMEM)
    return pl.pallas_call(
        spatial_kernel,
        out_shape=[jax.ShapeDtypeStruct(x.shape, BF16), jax.ShapeDtypeStruct((2, depth), F32)],
        in_specs=[whole, whole],
        out_specs=[whole, whole],
        scratch_shapes=[
            pltpu.VMEM((seq, depth), BF16),
            pltpu.VMEM((seq, depth), BF16),
            pltpu.VMEM((depth, seq), BF16),
            pltpu.VMEM((depth + ONES, seq), BF16),
            pltpu.VMEM((seq, seq), BF16),
            pltpu.VMEM((seq, seq), BF16),
            pltpu.VMEM((depth + ONES, BLOCK), F32),
            pltpu.VMEM((depth, seq), BF16),
            pltpu.VMEM((seq, depth), BF16),
            pltpu.VMEM((depth, BLOCK), F32),
        ],
        compiler_params=params(40),
        cost_estimate=cost(6 * 2 * seq * seq * depth, 4 << 20, seq * seq),
        name="spatial_attention",
    )(gains, x)


def shift(step):
    return [(i, ((i // 4 + step[0]) % 2) * 4 + (i % 4 + step[1]) % 4) for i in range(8)]


def exchange(parts, back):
    sent = [parts[0]]
    for part, step in zip(parts[1:], STEPS[1:]):
        step = tuple(-s for s in step) if back else step
        sent.append(lax.ppermute(part, "frame", shift(step)))
    return sent


def total(x):
    for axis, size in (("frame", 8), ("tile", 32)):
        bit = 1
        while bit < size:
            x = x + lax.ppermute(x, axis, [(i, i ^ bit) for i in range(size)])
            bit *= 2
    return x


def local(query_s, key_s, value_s, grad_out_s, query_t, key_t, value_t, grad_out_t, gains):
    frames = query_s.shape[0]
    me = lax.axis_index("frame")
    at = jnp.stack([((me // 4 + dy) % 2) * 4 + (me % 4 + dx) % 4 for dy, dx in STEPS]).astype(jnp.int32)

    sent = pack_s((query_s, key_s, value_s, grad_out_s))
    items = lax.all_to_all(sent, "tile", split_axis=0, concat_axis=0, tiled=True)

    parts = exchange(pack_t(at, (query_t, key_t, value_t, grad_out_t)), False)
    parts, grads_t = temporal(gains, parts)
    outs_t = unpack_t(at, exchange(parts, True))

    res, grads_s = spatial(gains, items)
    home = lax.all_to_all(res, "tile", split_axis=0, concat_axis=0, tiled=True)
    outs_s = unpack_s(home, frames)

    gain_grads = total(jnp.concatenate([grads_s, grads_t], axis=0))
    return (*outs_s, *outs_t, gain_grads)


def solution(mesh):
    split = P("frame", "tile", None)
    return jax.shard_map(
        local,
        mesh=mesh,
        in_specs=(split,) * 8 + (P(),),
        out_specs=(split,) * 8 + (P(),),
        check_vma=False,
    )
```

```python
import functools

import jax
import jax.numpy as jnp
from jax import lax
from jax.experimental import pallas as pl
from jax.experimental.pallas import tpu as pltpu
from jax.sharding import PartitionSpec as P

HEADS = 16
HEAD_DIM = 128
EPS = 1e-06
SCALE = HEAD_DIM**-0.5
LOG2E = 1.4426950408889634
BF16 = jnp.bfloat16
F32 = jnp.float32
SEQ = 2048
BLOCK = 1024
ONES = 16
TEMPORAL_FLOPS = 23 * 10**9
XSTEPS = (1, 3, 2)


def dot(a, b, ca, cb):
    return lax.dot_general(a, b, (((ca,), (cb,)), ((), ())), preferred_element_type=F32)


def params(mib):
    return pltpu.CompilerParams(vmem_limit_bytes=mib << 20)


def cost(flops, nbytes, trans=0):
    return pl.CostEstimate(flops=flops, bytes_accessed=nbytes, transcendentals=trans)


def inverse_rms(xf):
    return lax.rsqrt(jnp.mean(xf * xf, axis=-1, keepdims=True) + EPS)


def norm_back(grad_hat, x, gain):
    xf = x.astype(F32)
    inverse = inverse_rms(xf)
    unit = xf * inverse
    scaled = grad_hat * gain
    dgain = jnp.sum(grad_hat * unit, axis=0, keepdims=True)
    dx = inverse * (scaled - unit * jnp.mean(scaled * unit, axis=-1, keepdims=True))
    return dx.astype(BF16), dgain


def pack_s_kernel(q_ref, k_ref, v_ref, d_ref, o_ref):
    heads = o_ref.shape[1]
    for a, ref in enumerate((q_ref, k_ref, v_ref, d_ref)):
        for f in range(2):
            for h in range(heads):
                o_ref[f, h, a] = ref[f, :, h * HEAD_DIM : (h + 1) * HEAD_DIM]


def pack_s(arrays):
    frames, places, width = arrays[0].shape
    group = 8
    out = pl.pallas_call(
        pack_s_kernel,
        out_shape=jax.ShapeDtypeStruct((frames, HEADS, 4, places, HEAD_DIM), BF16),
        grid=(HEADS // group,),
        in_specs=[pl.BlockSpec((frames, places, group * HEAD_DIM), lambda i: (0, 0, i))] * 4,
        out_specs=pl.BlockSpec((frames, group, 4, places, HEAD_DIM), lambda i: (0, i, 0, 0, 0)),
        compiler_params=params(60),
        cost_estimate=cost(0, 4 << 20),
        name="pack_spatial",
    )(*arrays)
    return out.reshape(frames * HEADS, 4, places, HEAD_DIM)


def unpack_s_kernel(x_ref, *out_refs):
    heads = x_ref.shape[1]
    for a, ref in enumerate(out_refs):
        for f in range(2):
            for h in range(heads):
                ref[f, :, h * HEAD_DIM : (h + 1) * HEAD_DIM] = x_ref[f, h, a]


def unpack_s(x, frames):
    places = x.shape[2]
    group = 4
    return pl.pallas_call(
        unpack_s_kernel,
        out_shape=[jax.ShapeDtypeStruct((frames, places, HEADS * HEAD_DIM), BF16)] * 4,
        grid=(HEADS // group,),
        in_specs=[pl.BlockSpec((frames, group, 4, places, HEAD_DIM), lambda i: (0, i, 0, 0, 0))],
        out_specs=[pl.BlockSpec((frames, places, group * HEAD_DIM), lambda i: (0, 0, i))] * 4,
        compiler_params=params(16),
        cost_estimate=cost(0, 4 << 20),
        name="unpack_spatial",
    )(x.reshape(frames, HEADS, 4, places, HEAD_DIM))


def lanes_of(at_ref, j, width):
    return pl.ds(pl.multiple_of(at_ref[j] * width, width), width)


def pack_t_kernel(at_ref, q_ref, k_ref, v_ref, d_ref, *out_refs):
    width = out_refs[0].shape[-1]
    slots = [ref.at[i] for ref in out_refs for i in range(ref.shape[0])]
    for j, slot in enumerate(slots):
        lanes = lanes_of(at_ref, j, width)
        for a, ref in enumerate((q_ref, k_ref, v_ref, d_ref)):
            slot[a] = ref[:, :, lanes]


def pack_t(at, arrays, sizes):
    frames, places, width = arrays[0].shape
    part = width // 8
    return pl.pallas_call(
        pack_t_kernel,
        out_shape=[jax.ShapeDtypeStruct((n, 4, frames, places, part), BF16) for n in sizes],
        grid_spec=pltpu.PrefetchScalarGridSpec(
            num_scalar_prefetch=1,
            grid=(frames,),
            in_specs=[pl.BlockSpec((1, places, width // 2), lambda f, at: (f, 0, at[4]))] * 4,
            out_specs=[pl.BlockSpec((n, 4, 1, places, part), lambda f, at: (0, 0, f, 0, 0)) for n in sizes],
        ),
        compiler_params=params(60),
        cost_estimate=cost(0, 2 << 20),
        name="pack_temporal",
    )(at, *arrays)


def unpack_t_kernel(at_ref, grads_ref, *refs):
    parts, outs, grads_out = refs[:8], refs[8:12], refs[12]
    grads_out[...] = grads_ref[...]
    width = parts[0].shape[-1]
    for j, part in enumerate(parts):
        lanes = lanes_of(at_ref, j, width)
        for a, out in enumerate(outs):
            out[:, :, lanes] = part[0, a]


def unpack_t(at, grads, parts):
    _, _, frames, places, part = parts[0].shape
    return pl.pallas_call(
        unpack_t_kernel,
        out_shape=[jax.ShapeDtypeStruct((frames, places, part * 8), BF16)] * 4
        + [jax.ShapeDtypeStruct(grads.shape, F32)],
        in_specs=[pl.BlockSpec(memory_space=pltpu.SMEM)] + [pl.BlockSpec(memory_space=pltpu.VMEM)] * 9,
        out_specs=[pl.BlockSpec(memory_space=pltpu.VMEM)] * 5,
        compiler_params=params(16),
        cost_estimate=cost(0, 4 << 20),
        name="unpack_temporal",
    )(at, grads, *parts)


def temporal_kernel(gains_ref, *refs):
    ins = [ref.at[0] for ref in refs[:8]]
    outs = [ref.at[0] for ref in refs[8:13]] + [refs[9].at[i] for i in range(1, 4)]
    dgain_ref = refs[13]
    _, frames, places, width = ins[0].shape
    rows = 8 * frames * 16
    gain_q, gain_k = gains_ref[2:3, :], gains_ref[3:4, :]
    row = lax.broadcasted_iota(jnp.int32, (rows, rows), 0)
    column = lax.broadcasted_iota(jnp.int32, (rows, rows), 1)
    same = (row % 16) == (column % 16)
    dgain_ref[...] = jnp.zeros_like(dgain_ref)

    def step(block, _):
        at = pl.ds(pl.multiple_of(block * 16, 16), 16)
        for h in range(width // HEAD_DIM):
            lanes = slice(h * HEAD_DIM, (h + 1) * HEAD_DIM)

            def take(a):
                return jnp.concatenate([ref[a, f, at, lanes] for ref in ins for f in range(frames)], axis=0)

            query, key, value, dout = take(0), take(1), take(2), take(3)
            qf, kf = query.astype(F32), key.astype(F32)
            qh = (qf * inverse_rms(qf) * gain_q).astype(BF16)
            kh = (kf * inverse_rms(kf) * gain_k).astype(BF16)
            expo = jnp.where(same, jnp.exp(dot(qh, kh, 1, 1) * SCALE), 0.0)
            probs = expo / jnp.sum(expo, axis=-1, keepdims=True)
            probs_b = probs.astype(BF16)
            out = dot(probs_b, value, 1, 0)
            dprob = dot(dout, value, 1, 1)
            delta = jnp.sum(dout.astype(F32) * out, axis=-1, keepdims=True)
            dscore = (probs * (dprob - delta)).astype(BF16)
            dqh = dot(dscore, kh, 1, 0) * SCALE
            dkh = dot(dscore, qh, 0, 0) * SCALE
            dvalue = dot(probs_b, dout, 0, 0)
            dquery, dgain_q = norm_back(dqh, query, gain_q)
            dkey, dgain_k = norm_back(dkh, key, gain_k)
            dgain_ref[0:1, :] += dgain_q
            dgain_ref[1:2, :] += dgain_k
            for a, res in enumerate((out.astype(BF16), dquery, dkey, dvalue.astype(BF16))):
                for j, ref in enumerate(outs):
                    for f in range(frames):
                        first = (j * frames + f) * 16
                        ref[a, f, at, lanes] = res[first : first + 16]
        return 0

    lax.fori_loop(0, places // 16, step, 0, unroll=True)


def temporal(gains, parts):
    whole = pl.BlockSpec(memory_space=pltpu.VMEM)
    shape = parts[0].shape
    sizes = (1, 4, 1, 1, 1)
    res = pl.pallas_call(
        temporal_kernel,
        out_shape=[jax.ShapeDtypeStruct((n, *shape[1:]), BF16) for n in sizes]
        + [jax.ShapeDtypeStruct((2, HEAD_DIM), F32)],
        in_specs=[whole] * 9,
        out_specs=[whole] * 6,
        compiler_params=params(24),
        cost_estimate=cost(TEMPORAL_FLOPS, 4 << 20, 8 * 65536),
        name="temporal_attention",
    )(gains, *parts)
    return res[0], res[1], res[2:5], res[5]


def spatial_kernel(
    gains_ref, grads_t_ref, x_ref, out_ref, dgain_ref, qh, kh, kh_t, v_t, expo, dscore, out_t, dp_t, dp_n, dq_t
):
    tiles, _, places, depth = x_ref.shape
    seq = tiles * places
    per = BLOCK // places
    gain_q, gain_k = gains_ref[0:1, :], gains_ref[1:2, :]

    def rows_of(b):
        return pl.ds(pl.multiple_of(b * BLOCK, BLOCK), BLOCK)

    def read(a, b):
        return x_ref[pl.ds(b * per, per), a].reshape(BLOCK, depth)

    def write(a, b, value):
        out_ref[pl.ds(b * per, per), a] = value.astype(BF16).reshape(per, places, depth)

    def prepare(b, _):
        rows = rows_of(b)
        qf = read(0, b).astype(F32)
        qh[rows, :] = (qf * inverse_rms(qf) * gain_q).astype(BF16)
        kf = read(1, b).astype(F32)
        k_hat = (kf * inverse_rms(kf) * gain_k).astype(BF16)
        kh[rows, :] = k_hat
        kh_t[:, rows] = k_hat.T
        v_t[0:depth, rows] = read(2, b).T
        v_t[depth:, rows] = jnp.ones((ONES, BLOCK), BF16)
        return 0

    lax.fori_loop(0, seq // BLOCK, prepare, 0)

    def forward(b, _):
        rows = rows_of(b)
        q_b = qh[rows, :]
        for c in range(seq // BLOCK):
            keys = slice(c * BLOCK, (c + 1) * BLOCK)
            scores = dot(kh[keys, :], q_b, 1, 1)
            expo[keys, rows] = jnp.exp2(scores * (SCALE * LOG2E)).astype(BF16)
        out_t[...] = dot(v_t[...], expo[:, rows], 1, 0)
        inverse = 1.0 / out_t[depth : depth + 1, :]
        o_t = out_t[0:depth, :] * inverse
        write(0, b, o_t.astype(BF16).T)
        d_t = (read(3, b).T.astype(F32) * inverse).astype(BF16)
        delta = jnp.sum(d_t.astype(F32) * o_t, axis=0, keepdims=True)
        dp_t[:, rows] = d_t
        dp_n[rows, :] = d_t.T
        for c in range(seq // BLOCK):
            keys = slice(c * BLOCK, (c + 1) * BLOCK)
            value = x_ref[c * per : (c + 1) * per, 2].reshape(BLOCK, depth)
            grad = dot(value, d_t, 1, 0)
            dscore[keys, rows] = (expo[keys, rows].astype(F32) * (grad - delta)).astype(BF16)
        dq_t[...] = dot(kh_t[...], dscore[:, rows], 1, 0) * SCALE
        dquery, dgain = norm_back(dq_t[...].T, read(0, b), gain_q)
        write(1, b, dquery)
        dgain_ref[0:1, :] += dgain
        return 0

    dgain_ref[0:2, :] = jnp.zeros((2, depth), F32)
    dgain_ref[2:4, :] = grads_t_ref[...]
    lax.fori_loop(0, seq // BLOCK, forward, 0)

    def backward(b, _):
        rows = rows_of(b)
        dkh = dot(dscore[rows, :], qh[...], 1, 0) * SCALE
        dkey, dgain = norm_back(dkh, read(1, b), gain_k)
        write(2, b, dkey)
        dgain_ref[1:2, :] += dgain
        write(3, b, dot(expo[rows, :], dp_n[...], 1, 0))
        return 0

    lax.fori_loop(0, seq // BLOCK, backward, 0)


def spatial(gains, grads_t, x):
    tiles, _, places, depth = x.shape
    seq = tiles * places
    whole = pl.BlockSpec(memory_space=pltpu.VMEM)
    return pl.pallas_call(
        spatial_kernel,
        out_shape=[jax.ShapeDtypeStruct(x.shape, BF16), jax.ShapeDtypeStruct((4, depth), F32)],
        in_specs=[whole, whole, whole],
        out_specs=[whole, whole],
        scratch_shapes=[
            pltpu.VMEM((seq, depth), BF16),
            pltpu.VMEM((seq, depth), BF16),
            pltpu.VMEM((depth, seq), BF16),
            pltpu.VMEM((depth + ONES, seq), BF16),
            pltpu.VMEM((seq, seq), BF16),
            pltpu.VMEM((seq, seq), BF16),
            pltpu.VMEM((depth + ONES, BLOCK), F32),
            pltpu.VMEM((depth, seq), BF16),
            pltpu.VMEM((seq, depth), BF16),
            pltpu.VMEM((depth, BLOCK), F32),
        ],
        compiler_params=params(36),
        cost_estimate=cost(6 * 2 * seq * seq * depth, 4 << 20, seq * seq),
        name="spatial_attention",
    )(gains, grads_t, x)


def after_kernel(x_ref, *refs):
    pass


def after(x, others):
    anywhere = pl.BlockSpec(memory_space=pl.ANY)
    return pl.pallas_call(
        after_kernel,
        out_shape=jax.ShapeDtypeStruct(x.shape, x.dtype),
        in_specs=[anywhere] * (1 + len(others)),
        out_specs=anywhere,
        input_output_aliases={0: 0},
        compiler_params=params(1),
        cost_estimate=cost(0, 1024),
        name="after",
    )(x, *others)


def over_tile(x):
    count, arrays, places, depth = x.shape
    x = x.reshape(count, arrays * places, depth)
    return lax.all_to_all(x, "tile", split_axis=0, concat_axis=0, tiled=True).reshape(count, arrays, places, depth)


def along_x(x, step):
    return lax.ppermute(x, "frame", [(i, i // 4 * 4 + (i + step) % 4) for i in range(8)])


def across(x):
    return lax.ppermute(x, "frame", [(i, (i + 4) % 8) for i in range(8)])


def from_partner(x, axis, bit):
    size = 8 if axis == "frame" else 32
    return lax.ppermute(x, axis, [(i, i ^ bit) for i in range(size)])


def total_off_z(x):
    for axis, bit in (("frame", 1), ("frame", 2), ("frame", 4), ("tile", 1), ("tile", 2)):
        x = x + from_partner(x, axis, bit)
    return x


def total_z(x):
    got = []
    for near, far in ((None, 4), (1, 5), (2, 6), (3, 7)):
        perm = [(i, i ^ (4 * far)) for i in range(1, 32, 2)]
        if near is not None:
            perm += [(i, i ^ (4 * near)) for i in range(0, 32, 2)]
        got.append(lax.ppermute(x, "tile", perm))
    got[0] = jnp.where(lax.axis_index("tile") % 2 == 0, x, got[0])
    half = (got[0] + got[1]) + (got[2] + got[3])
    return half + from_partner(half, "tile", 1)


def local(query_s, key_s, value_s, grad_out_s, query_t, key_t, value_t, grad_out_t, gains):
    frames = query_s.shape[0]
    me = lax.axis_index("frame")
    row, x = me // 4, me % 4
    order = (0, *XSTEPS)
    places = [(x + step) % 4 for step in order]
    at_here = jnp.stack(places + [row]).astype(jnp.int32)
    at_there = jnp.stack(places + [1 - row]).astype(jnp.int32)
    at_all = jnp.stack([4 * row + p for p in places] + [4 * (1 - row) + p for p in places]).astype(jnp.int32)
    given_t = (query_t, key_t, value_t, grad_out_t)

    (there,) = pack_t(at_there, given_t, (4,))
    there = across(there)
    sent = pack_s((query_s, key_s, value_s, grad_out_s))
    items = over_tile(sent)
    here = pack_t(at_here, given_t, (1, 1, 1, 1))
    parts = [here[0], there]
    for i, step in enumerate(XSTEPS):
        parts.append(along_x(here[i + 1], step))
    for i, step in enumerate(XSTEPS):
        parts.append(along_x(there[i + 1 : i + 2], step))

    own, there, here, grads_t = temporal(gains, parts)
    there = across(there)
    here = [along_x(part, -step) for part, step in zip(here, XSTEPS)]
    there_x = [along_x(there[i + 1 : i + 2], -step) for i, step in enumerate(XSTEPS)]

    res, grads = spatial(gains, grads_t, items)
    home = over_tile(after(res, [there, *here]))
    *outs_t, grads = unpack_t(at_all, total_off_z(grads), [own, *here, there, *there_x])
    gain_grads = total_z(grads)
    outs_s = unpack_s(home, frames)
    return (*outs_s, *outs_t, gain_grads)


def solution(mesh):
    split = P("frame", "tile", None)
    return jax.shard_map(
        local,
        mesh=mesh,
        in_specs=(split,) * 8 + (P(),),
        out_specs=(split,) * 8 + (P(),),
        check_vma=False,
    )
```

```python
import functools

import jax
import jax.numpy as jnp
from jax import lax
from jax.experimental import pallas as pl
from jax.experimental.pallas import tpu as pltpu
from jax.sharding import PartitionSpec as P

HEADS = 16
HEAD_DIM = 128
EPS = 1e-06
SCALE = HEAD_DIM**-0.5
LOG2E = 1.4426950408889634
BF16 = jnp.bfloat16
F32 = jnp.float32
SEQ = 2048
BLOCK = 1024
ONES = 16
TEMPORAL_FLOPS = 30 * 10**9
XSTEPS = (1, 3, 2)
TEMPORAL_MIB = 24
UNPACK_MIB = 24
TEMPORAL_ROWS = 32
TOGETHER = 4
HERE_FIRST = 3


def dot(a, b, ca, cb):
    return lax.dot_general(a, b, (((ca,), (cb,)), ((), ())), preferred_element_type=F32)


def params(mib):
    return pltpu.CompilerParams(vmem_limit_bytes=mib << 20)


def cost(flops, nbytes, trans=0):
    return pl.CostEstimate(flops=flops, bytes_accessed=nbytes, transcendentals=trans)


def inverse_rms(xf):
    return lax.rsqrt(jnp.mean(xf * xf, axis=-1, keepdims=True) + EPS)


def norm_back(grad_hat, x, gain):
    xf = x.astype(F32)
    inverse = inverse_rms(xf)
    unit = xf * inverse
    scaled = grad_hat * gain
    dgain = jnp.sum(grad_hat * unit, axis=0, keepdims=True)
    dx = inverse * (scaled - unit * jnp.mean(scaled * unit, axis=-1, keepdims=True))
    return dx.astype(BF16), dgain


def places_of_x(width):
    x = lax.rem(lax.axis_index("frame"), 4)
    return [pl.ds(pl.multiple_of(lax.rem(x + step, 4) * width, width), width) for step in (0, *XSTEPS)]


def row_lanes(other, width):
    row = lax.div(lax.axis_index("frame"), 4)
    row = 1 - row if other else row
    return pl.ds(pl.multiple_of(row * width, width), width)


def pack_kernel(*refs):
    far, near, there_refs, sent_ref = refs[:4], refs[4:8], refs[8:10], refs[10]
    far_in, near_in, there, sent, sem_far, sem_near, sem_there, sem_sent = refs[11:]
    frames, places, half = far_in.shape[1:]
    part = half // 4
    lanes = row_lanes(True, half)

    def fetch_far(a):
        return pltpu.make_async_copy(far[a].at[:, :, lanes], far_in.at[a], sem_far.at[a])

    def fetch_near(a, f):
        return pltpu.make_async_copy(near[a].at[f], near_in.at[a, f], sem_near.at[a, f])

    def send_there(a, i):
        pair = pl.ds(2 * i, 2)
        return pltpu.make_async_copy(there.at[pair, a], there_refs[i].at[:, a], sem_there.at[a, i])

    def send_sent(a, f):
        heads = pl.ds(f * HEADS, HEADS)
        return pltpu.make_async_copy(sent.at[heads, a], sent_ref.at[heads, a], sem_sent.at[a, f])

    for a in range(4):
        fetch_far(a).start()
    for a in range(4):
        for f in range(frames):
            fetch_near(a, f).start()
    spans = places_of_x(part)
    for a in range(4):
        fetch_far(a).wait()
        for i, span in enumerate(spans):
            there[i, a] = far_in[a, :, :, span]
        for i in range(2):
            send_there(a, i).start()
    for a in range(4):
        for f in range(frames):
            fetch_near(a, f).wait()
            for h in range(HEADS):
                sent[f * HEADS + h, a] = near_in[a, f, :, h * HEAD_DIM : (h + 1) * HEAD_DIM]
            send_sent(a, f).start()
    for a in range(4):
        for i in range(2):
            send_there(a, i).wait()
        for f in range(frames):
            send_sent(a, f).wait()


def pack(far, near):
    frames, places, width = near[0].shape
    there = (4, 4, frames, places, width // 8)
    sent = (frames * HEADS, 4, places, HEAD_DIM)
    anywhere = pl.BlockSpec(memory_space=pl.ANY)
    return pl.pallas_call(
        pack_kernel,
        out_shape=[jax.ShapeDtypeStruct((2, *there[1:]), BF16)] * 2 + [jax.ShapeDtypeStruct(sent, BF16)],
        in_specs=[anywhere] * 8,
        out_specs=[anywhere] * 3,
        scratch_shapes=[
            pltpu.VMEM((4, frames, places, width // 2), BF16),
            pltpu.VMEM((4, frames, places, width), BF16),
            pltpu.VMEM(there, BF16),
            pltpu.VMEM(sent, BF16),
            pltpu.SemaphoreType.DMA((4,)),
            pltpu.SemaphoreType.DMA((4, frames)),
            pltpu.SemaphoreType.DMA((4, 2)),
            pltpu.SemaphoreType.DMA((4, frames)),
        ],
        compiler_params=params(60),
        cost_estimate=cost(0, 6 << 20),
        name="pack",
    )(*far, *near)


def pack_here_kernel(q_ref, k_ref, v_ref, d_ref, *refs):
    outs, held, sem = refs[:4], refs[4], refs[5]
    lanes = row_lanes(False, held.shape[-1])
    copies = [
        pltpu.make_async_copy(ref.at[:, :, lanes], held.at[a], sem.at[a])
        for a, ref in enumerate((q_ref, k_ref, v_ref, d_ref))
    ]
    for copy in copies:
        copy.start()
    spans = places_of_x(held.shape[-1] // 4)
    for a, copy in enumerate(copies):
        copy.wait()
        for out, span in zip(outs, spans):
            out[0, a] = held[a, :, :, span]


def pack_here(arrays):
    frames, places, width = arrays[0].shape
    return pl.pallas_call(
        pack_here_kernel,
        out_shape=[jax.ShapeDtypeStruct((1, 4, frames, places, width // 8), BF16)] * 4,
        in_specs=[pl.BlockSpec(memory_space=pl.ANY)] * 4,
        out_specs=[pl.BlockSpec(memory_space=pltpu.VMEM)] * 4,
        scratch_shapes=[pltpu.VMEM((4, frames, places, width // 2), BF16), pltpu.SemaphoreType.DMA((4,))],
        compiler_params=params(56),
        cost_estimate=cost(0, 2 << 20),
        name="pack_here",
    )(*arrays)


def unpack_s_kernel(x_ref, half_ref, other_ref, *out_refs):
    heads = x_ref.shape[1]
    out_refs[4][...] = half_ref[...] + other_ref[...]
    for a, ref in enumerate(out_refs[:4]):
        for f in range(2):
            for h in range(heads):
                ref[f, :, h * HEAD_DIM : (h + 1) * HEAD_DIM] = x_ref[f, h, a]


def unpack_s(x, halves, frames):
    places = x.shape[2]
    group = 4
    whole = pl.BlockSpec(halves[0].shape, lambda i: (0, 0))
    return pl.pallas_call(
        unpack_s_kernel,
        out_shape=[jax.ShapeDtypeStruct((frames, places, HEADS * HEAD_DIM), BF16)] * 4
        + [jax.ShapeDtypeStruct(halves[0].shape, F32)],
        grid=(HEADS // group,),
        in_specs=[pl.BlockSpec((frames, group, 4, places, HEAD_DIM), lambda i: (0, i, 0, 0, 0)), whole, whole],
        out_specs=[pl.BlockSpec((frames, places, group * HEAD_DIM), lambda i: (0, 0, i))] * 4 + [whole],
        compiler_params=params(16),
        cost_estimate=cost(0, 4 << 20),
        name="unpack_spatial",
    )(x.reshape(frames, HEADS, 4, places, HEAD_DIM), *halves)


def unpack_t_kernel(grads_ref, *refs):
    parts, outs, grads_out = refs[:8], refs[8:12], refs[12]
    half = outs[0].shape[-1] // 2
    part = half // 4
    grads_out[...] = grads_ref[...]
    row, x = lax.div(lax.axis_index("frame"), 4), lax.rem(lax.axis_index("frame"), 4)
    for j, ref in enumerate(parts):
        first = (1 - row if j >= 4 else row) * half + lax.rem(x + (0, *XSTEPS)[j % 4], 4) * part
        lanes = pl.ds(pl.multiple_of(first, part), part)
        for a, out in enumerate(outs):
            out[:, :, lanes] = ref[0, a]


def unpack_t(grads, parts):
    _, _, frames, places, part = parts[0].shape
    whole = pl.BlockSpec(grads.shape, lambda f: (0, 0))
    return pl.pallas_call(
        unpack_t_kernel,
        out_shape=[jax.ShapeDtypeStruct((frames, places, part * 8), BF16)] * 4
        + [jax.ShapeDtypeStruct(grads.shape, F32)],
        grid=(frames,),
        in_specs=[whole] + [pl.BlockSpec((1, 4, 1, places, part), lambda f: (0, 0, f, 0, 0))] * 8,
        out_specs=[pl.BlockSpec((1, places, part * 8), lambda f: (f, 0, 0))] * 4 + [whole],
        compiler_params=params(UNPACK_MIB),
        cost_estimate=cost(0, 4 << 20),
        name="unpack_temporal",
    )(grads, *parts)


def temporal_kernel(gains_ref, *refs):
    ins = [ref.at[0] for ref in refs[:8]]
    own, there, here, dgain_ref = refs[8], refs[9], refs[10:13], refs[13]
    there = [there.at[i] for i in range(4)]
    outs = [own.at[0], there[0]] + [ref.at[0] for ref in here] + there[1:]
    _, frames, places, width = ins[0].shape
    rows = 8 * frames * 16
    gain_q, gain_k = gains_ref[2:3, :], gains_ref[3:4, :]

    @pl.when(pl.program_id(0) == 0)
    def _():
        dgain_ref[...] = jnp.zeros_like(dgain_ref)

    row = lax.broadcasted_iota(jnp.int32, (rows, rows), 0)
    column = lax.broadcasted_iota(jnp.int32, (rows, rows), 1)
    same = (row % 16) == (column % 16)

    spots = [
        (slice(first, first + 16), slice(h, h + HEAD_DIM))
        for first in range(0, places, 16)
        for h in range(0, width, HEAD_DIM)
    ]
    for first in range(0, len(spots), TOGETHER):
        temporal_spots(spots[first : first + TOGETHER], ins, outs, dgain_ref, gain_q, gain_k, same)


def temporal_spots(spots, ins, outs, dgain_ref, gain_q, gain_k, same):
    frames = ins[0].shape[1]

    def take(a):
        return [jnp.concatenate([ref[a, f, *spot] for ref in ins for f in range(frames)], axis=0) for spot in spots]

    def each(f, *lists):
        return [f(*items) for items in zip(*lists)]

    def put(a, results):
        for spot, result in zip(spots, results):
            result = result.astype(BF16)
            for j, ref in enumerate(outs):
                for f in range(frames):
                    first = (j * frames + f) * 16
                    ref[a, f, *spot] = result[first : first + 16]

    def hat(x, gain):
        xf = x.astype(F32)
        return (xf * inverse_rms(xf) * gain).astype(BF16)

    query, key, value, dout = take(0), take(1), take(2), take(3)
    qh = each(lambda x: hat(x, gain_q), query)
    kh = each(lambda x: hat(x, gain_k), key)
    expo = each(lambda q, k: jnp.where(same, jnp.exp(dot(q, k, 1, 1) * SCALE), 0.0), qh, kh)
    probs = each(lambda e: e / jnp.sum(e, axis=-1, keepdims=True), expo)
    probs_b = each(lambda p: p.astype(BF16), probs)
    out = each(lambda p, v: dot(p, v, 1, 0), probs_b, value)
    dprob = each(lambda d, v: dot(d, v, 1, 1), dout, value)
    put(0, out)
    delta = each(lambda d, o: jnp.sum(d.astype(F32) * o, axis=-1, keepdims=True), dout, out)
    dscore = each(lambda p, dp, d: (p * (dp - d)).astype(BF16), probs, dprob, delta)
    put(3, each(lambda p, d: dot(p, d, 0, 0), probs_b, dout))
    dqh = each(lambda ds, k: dot(ds, k, 1, 0) * SCALE, dscore, kh)
    dkh = each(lambda ds, q: dot(ds, q, 0, 0) * SCALE, dscore, qh)
    for a, grads, given, gain in ((1, dqh, query, gain_q), (2, dkh, key, gain_k)):
        back = each(lambda g, x, gain=gain: norm_back(g, x, gain), grads, given)
        put(a, [dx for dx, _ in back])
        dgain_ref[a - 1 : a, :] += sum(dgain for _, dgain in back)


def temporal(gains, parts):
    _, arrays, frames, places, width = parts[0].shape
    sizes = (1, 4, 1, 1, 1)

    def block(n):
        return pl.BlockSpec((n, arrays, frames, TEMPORAL_ROWS, width), lambda i: (0, 0, 0, i, 0))

    res = pl.pallas_call(
        temporal_kernel,
        out_shape=[jax.ShapeDtypeStruct((n, arrays, frames, places, width), BF16) for n in sizes]
        + [jax.ShapeDtypeStruct((2, HEAD_DIM), F32)],
        grid=(places // TEMPORAL_ROWS,),
        in_specs=[pl.BlockSpec(gains.shape, lambda i: (0, 0))] + [block(1)] * 8,
        out_specs=[block(n) for n in sizes] + [pl.BlockSpec((2, HEAD_DIM), lambda i: (0, 0))],
        compiler_params=params(TEMPORAL_MIB),
        cost_estimate=cost(TEMPORAL_FLOPS, 4 << 20, 8 * 65536),
        name="temporal_attention",
    )(gains, *parts)
    return res[0], res[1], res[2:5], res[5]


def spatial_kernel(
    gains_ref, grads_t_ref, x_ref, home_ref, dgain_ref, qh, kh, kh_t, v_t, expo, dscore, out_t, dp_t, dp_n, dq_t, out_ref, sem
):
    tiles, _, places, depth = x_ref.shape
    seq = tiles * places
    per = BLOCK // places
    gain_q, gain_k = gains_ref[0:1, :], gains_ref[1:2, :]

    def rows_of(b):
        return pl.ds(pl.multiple_of(b * BLOCK, BLOCK), BLOCK)

    def read(a, b):
        return x_ref[pl.ds(b * per, per), a].reshape(BLOCK, depth)

    def write(a, b, value):
        out_ref[pl.ds(b * per, per), a] = value.astype(BF16).reshape(per, places, depth)

    def prepare(b, _):
        rows = rows_of(b)
        qf = read(0, b).astype(F32)
        qh[rows, :] = (qf * inverse_rms(qf) * gain_q).astype(BF16)
        kf = read(1, b).astype(F32)
        k_hat = (kf * inverse_rms(kf) * gain_k).astype(BF16)
        kh[rows, :] = k_hat
        kh_t[:, rows] = k_hat.T
        v_t[0:depth, rows] = read(2, b).T
        v_t[depth:, rows] = jnp.ones((ONES, BLOCK), BF16)
        return 0

    lax.fori_loop(0, seq // BLOCK, prepare, 0)

    def forward(b, _):
        rows = rows_of(b)
        q_b = qh[rows, :]
        for c in range(seq // BLOCK):
            keys = slice(c * BLOCK, (c + 1) * BLOCK)
            scores = dot(kh[keys, :], q_b, 1, 1)
            expo[keys, rows] = jnp.exp2(scores * (SCALE * LOG2E)).astype(BF16)
        out_t[...] = dot(v_t[...], expo[:, rows], 1, 0)
        inverse = 1.0 / out_t[depth : depth + 1, :]
        o_t = out_t[0:depth, :] * inverse
        write(0, b, o_t.astype(BF16).T)
        d_t = (read(3, b).T.astype(F32) * inverse).astype(BF16)
        delta = jnp.sum(d_t.astype(F32) * o_t, axis=0, keepdims=True)
        dp_t[:, rows] = d_t
        dp_n[rows, :] = d_t.T
        for c in range(seq // BLOCK):
            keys = slice(c * BLOCK, (c + 1) * BLOCK)
            value = x_ref[c * per : (c + 1) * per, 2].reshape(BLOCK, depth)
            grad = dot(value, d_t, 1, 0)
            dscore[keys, rows] = (expo[keys, rows].astype(F32) * (grad - delta)).astype(BF16)
        dq_t[...] = dot(kh_t[...], dscore[:, rows], 1, 0) * SCALE
        dquery, dgain = norm_back(dq_t[...].T, read(0, b), gain_q)
        write(1, b, dquery)
        dgain_ref[0:1, :] += dgain
        sending(b, 0).start()
        return 0

    def sending(b, phase):
        part = (pl.ds(b * per, per), pl.ds(2 * phase, 2))
        return pltpu.make_async_copy(out_ref.at[part], home_ref.at[part], sem.at[phase, b])

    dgain_ref[0:2, :] = jnp.zeros((2, depth), F32)
    dgain_ref[2:4, :] = grads_t_ref[...]
    lax.fori_loop(0, seq // BLOCK, forward, 0)

    def backward(b, _):
        rows = rows_of(b)
        dkh = dot(dscore[rows, :], qh[...], 1, 0) * SCALE
        dkey, dgain = norm_back(dkh, read(1, b), gain_k)
        write(2, b, dkey)
        dgain_ref[1:2, :] += dgain
        write(3, b, dot(expo[rows, :], dp_n[...], 1, 0))
        sending(b, 1).start()
        return 0

    lax.fori_loop(0, seq // BLOCK, backward, 0)
    for phase in range(2):
        for b in range(seq // BLOCK):
            sending(b, phase).wait()


def spatial(gains, grads_t, x):
    tiles, _, places, depth = x.shape
    seq = tiles * places
    whole = pl.BlockSpec(memory_space=pltpu.VMEM)
    return pl.pallas_call(
        spatial_kernel,
        out_shape=[jax.ShapeDtypeStruct(x.shape, BF16), jax.ShapeDtypeStruct((4, depth), F32)],
        in_specs=[whole, whole, whole],
        out_specs=[pl.BlockSpec(memory_space=pl.ANY), whole],
        scratch_shapes=[
            pltpu.VMEM((seq, depth), BF16),
            pltpu.VMEM((seq, depth), BF16),
            pltpu.VMEM((depth, seq), BF16),
            pltpu.VMEM((depth + ONES, seq), BF16),
            pltpu.VMEM((seq, seq), BF16),
            pltpu.VMEM((seq, seq), BF16),
            pltpu.VMEM((depth + ONES, BLOCK), F32),
            pltpu.VMEM((depth, seq), BF16),
            pltpu.VMEM((seq, depth), BF16),
            pltpu.VMEM((depth, BLOCK), F32),
            pltpu.VMEM(x.shape, BF16),
            pltpu.SemaphoreType.DMA((2, seq // BLOCK)),
        ],
        compiler_params=params(36),
        cost_estimate=cost(6 * 2 * seq * seq * depth, 4 << 20, seq * seq),
        name="spatial_attention",
    )(gains, grads_t, x)


def after_kernel(x_ref, *refs):
    pass


def after(x, others):
    anywhere = pl.BlockSpec(memory_space=pl.ANY)
    return pl.pallas_call(
        after_kernel,
        out_shape=jax.ShapeDtypeStruct(x.shape, x.dtype),
        in_specs=[anywhere] * (1 + len(others)),
        out_specs=anywhere,
        input_output_aliases={0: 0},
        compiler_params=params(1),
        cost_estimate=cost(0, 1024),
        name="after",
    )(x, *others)


def over_tile(x):
    count, arrays, places, depth = x.shape
    x = x.reshape(count, arrays * places, depth)
    return lax.all_to_all(x, "tile", split_axis=0, concat_axis=0, tiled=True).reshape(count, arrays, places, depth)


def along_x(x, step):
    return lax.ppermute(x, "frame", [(i, i // 4 * 4 + (i + step) % 4) for i in range(8)])


def across(x):
    return lax.ppermute(x, "frame", [(i, (i + 4) % 8) for i in range(8)])


def three_of(there):
    return [there[0][1:], there[1][:1], there[1][1:]]


def from_partner(x, axis, bit):
    size = 8 if axis == "frame" else 32
    return lax.ppermute(x, axis, [(i, i ^ bit) for i in range(size)])


def total_off_z(x):
    for axis, bit in (("frame", 1), ("frame", 2), ("frame", 4), ("tile", 1), ("tile", 2)):
        x = x + from_partner(x, axis, bit)
    return x


def total_z(x):
    got = []
    for near, far in ((None, 4), (1, 5), (2, 6), (3, 7)):
        perm = [(i, i ^ (4 * far)) for i in range(1, 32, 2)]
        if near is not None:
            perm += [(i, i ^ (4 * near)) for i in range(0, 32, 2)]
        got.append(lax.ppermute(x, "tile", perm))
    got[0] = jnp.where(lax.axis_index("tile") % 2 == 0, x, got[0])
    half = (got[0] + got[1]) + (got[2] + got[3])
    return half, from_partner(half, "tile", 1)


def local(query_s, key_s, value_s, grad_out_s, query_t, key_t, value_t, grad_out_t, gains):
    frames = query_s.shape[0]
    given_t = (query_t, key_t, value_t, grad_out_t)

    *there, sent = pack(given_t, (query_s, key_s, value_s, grad_out_s))
    there = [across(pair) for pair in there]
    items = over_tile(sent)
    here = pack_here(given_t)
    parts = [here[0], there[0]]
    for part, step in zip(here[1:], XSTEPS):
        parts.append(along_x(part, step))
    for part, step in zip(three_of(there), XSTEPS):
        parts.append(along_x(part, step))

    own, there, here, grads_t = temporal(gains, parts)
    there = across(there)
    here = [along_x(part, -step) for part, step in zip(here, XSTEPS)]
    there_x = [along_x(there[i + 1 : i + 2], -step) for i, step in enumerate(XSTEPS)]

    res, grads = spatial(gains, grads_t, items)
    home = over_tile(after(res, [there, *here[:HERE_FIRST]]))
    *outs_t, grads = unpack_t(total_off_z(grads), [own, *here, there, *there_x])
    *outs_s, gain_grads = unpack_s(home, total_z(grads), frames)
    return (*outs_s, *outs_t, gain_grads)


def solution(mesh):
    split = P("frame", "tile", None)
    return jax.shard_map(
        local,
        mesh=mesh,
        in_specs=(split,) * 8 + (P(),),
        out_specs=(split,) * 8 + (P(),),
        check_vma=False,
    )
```

```python
import functools

import jax
import jax.numpy as jnp
from jax import lax
from jax.experimental import pallas as pl
from jax.experimental.pallas import tpu as pltpu
from jax.sharding import PartitionSpec as P

HEADS = 16
HEAD_DIM = 128
EPS = 1e-06
SCALE = HEAD_DIM**-0.5
LOG2E = 1.4426950408889634
BF16 = jnp.bfloat16
F32 = jnp.float32
SEQ = 2048
BLOCK = 1024
ONES = 16
TEMPORAL_FLOPS = 30 * 10**9
XSTEPS = (1, 3, 2)
TEMPORAL_MIB = 24
UNPACK_MIB = 24
TEMPORAL_ROWS = 32
TOGETHER = 4
HERE_FIRST = 3


def dot(a, b, ca, cb):
    return lax.dot_general(a, b, (((ca,), (cb,)), ((), ())), preferred_element_type=F32)


def params(mib):
    return pltpu.CompilerParams(vmem_limit_bytes=mib << 20)


def cost(flops, nbytes, trans=0):
    return pl.CostEstimate(flops=flops, bytes_accessed=nbytes, transcendentals=trans)


def inverse_rms(xf):
    return lax.rsqrt(jnp.mean(xf * xf, axis=-1, keepdims=True) + EPS)


def norm_back(grad_hat, x, gain):
    xf = x.astype(F32)
    inverse = inverse_rms(xf)
    unit = xf * inverse
    scaled = grad_hat * gain
    dgain = jnp.sum(grad_hat * unit, axis=0, keepdims=True)
    dx = inverse * (scaled - unit * jnp.mean(scaled * unit, axis=-1, keepdims=True))
    return dx.astype(BF16), dgain


def places_of_x(width):
    x = lax.rem(lax.axis_index("frame"), 4)
    return [pl.ds(pl.multiple_of(lax.rem(x + step, 4) * width, width), width) for step in (0, *XSTEPS)]


def row_lanes(other, width):
    row = lax.div(lax.axis_index("frame"), 4)
    row = 1 - row if other else row
    return pl.ds(pl.multiple_of(row * width, width), width)


def pack_kernel(*refs):
    far, near, there_ref, sent_ref = refs[:4], refs[4:8], refs[8], refs[9]
    far_in, near_in, there, sent, sem_far, sem_near, sem_there, sem_sent = refs[10:]
    frames, places, half = far_in.shape[1:]
    part = half // 4
    lanes = row_lanes(True, half)

    def fetch_far(a):
        return pltpu.make_async_copy(far[a].at[:, :, lanes], far_in.at[a], sem_far.at[a])

    def fetch_near(a, f):
        return pltpu.make_async_copy(near[a].at[f], near_in.at[a, f], sem_near.at[a, f])

    def send_there(a):
        return pltpu.make_async_copy(there.at[:, a], there_ref.at[:, a], sem_there.at[a])

    def send_sent(a, f):
        heads = pl.ds(f * HEADS, HEADS)
        return pltpu.make_async_copy(sent.at[heads, a], sent_ref.at[heads, a], sem_sent.at[a, f])

    for a in range(4):
        fetch_far(a).start()
    for a in range(4):
        for f in range(frames):
            fetch_near(a, f).start()
    spans = places_of_x(part)
    for a in range(4):
        fetch_far(a).wait()
        for i, span in enumerate(spans[1:]):
            there[i, a] = far_in[a, :, :, span]
        send_there(a).start()
    for a in range(4):
        for f in range(frames):
            fetch_near(a, f).wait()
            for h in range(HEADS):
                sent[f * HEADS + h, a] = near_in[a, f, :, h * HEAD_DIM : (h + 1) * HEAD_DIM]
            send_sent(a, f).start()
    for a in range(4):
        send_there(a).wait()
        for f in range(frames):
            send_sent(a, f).wait()


def pack(far, near):
    frames, places, width = near[0].shape
    there = (3, 4, frames, places, width // 8)
    sent = (frames * HEADS, 4, places, HEAD_DIM)
    anywhere = pl.BlockSpec(memory_space=pl.ANY)
    return pl.pallas_call(
        pack_kernel,
        out_shape=[jax.ShapeDtypeStruct(there, BF16)] + [jax.ShapeDtypeStruct(sent, BF16)],
        in_specs=[anywhere] * 8,
        out_specs=[anywhere] * 2,
        scratch_shapes=[
            pltpu.VMEM((4, frames, places, width // 2), BF16),
            pltpu.VMEM((4, frames, places, width), BF16),
            pltpu.VMEM(there, BF16),
            pltpu.VMEM(sent, BF16),
            pltpu.SemaphoreType.DMA((4,)),
            pltpu.SemaphoreType.DMA((4, frames)),
            pltpu.SemaphoreType.DMA((4,)),
            pltpu.SemaphoreType.DMA((4, frames)),
        ],
        compiler_params=params(60),
        cost_estimate=cost(0, 6 << 20),
        name="pack",
    )(*far, *near)


def pack_here_kernel(q_ref, k_ref, v_ref, d_ref, *refs):
    outs, far_out, held, sem, sem_far = refs[:4], refs[4], refs[5], refs[6], refs[7]
    lanes = row_lanes(False, held.shape[-1])
    part = held.shape[-1] // 4
    row, x = lax.div(lax.axis_index("frame"), 4), lax.rem(lax.axis_index("frame"), 4)
    far = pl.ds(pl.multiple_of(((1 - row) * 4 + x) * part, part), part)
    copies = [
        pltpu.make_async_copy(ref.at[:, :, lanes], held.at[a], sem.at[a])
        for a, ref in enumerate((q_ref, k_ref, v_ref, d_ref))
    ]
    far_copies = [
        pltpu.make_async_copy(ref.at[:, :, far], far_out.at[0, a], sem_far.at[a])
        for a, ref in enumerate((q_ref, k_ref, v_ref, d_ref))
    ]
    for copy in copies + far_copies:
        copy.start()
    spans = places_of_x(part)
    for a, copy in enumerate(copies):
        copy.wait()
        for out, span in zip(outs, spans):
            out[0, a] = held[a, :, :, span]
    for copy in far_copies:
        copy.wait()


def pack_here(arrays):
    frames, places, width = arrays[0].shape
    return pl.pallas_call(
        pack_here_kernel,
        out_shape=[jax.ShapeDtypeStruct((1, 4, frames, places, width // 8), BF16)] * 5,
        in_specs=[pl.BlockSpec(memory_space=pl.ANY)] * 4,
        out_specs=[pl.BlockSpec(memory_space=pltpu.VMEM)] * 5,
        scratch_shapes=[
            pltpu.VMEM((4, frames, places, width // 2), BF16),
            pltpu.SemaphoreType.DMA((4,)),
            pltpu.SemaphoreType.DMA((4,)),
        ],
        compiler_params=params(56),
        cost_estimate=cost(0, 2 << 20),
        name="pack_here",
    )(*arrays)


def unpack_s_kernel(x_ref, half_ref, other_ref, *out_refs):
    heads = x_ref.shape[1]
    out_refs[4][...] = half_ref[...] + other_ref[...]
    for a, ref in enumerate(out_refs[:4]):
        for f in range(2):
            for h in range(heads):
                ref[f, :, h * HEAD_DIM : (h + 1) * HEAD_DIM] = x_ref[f, h, a]


def unpack_s(x, halves, frames):
    places = x.shape[2]
    group = 4
    whole = pl.BlockSpec(halves[0].shape, lambda i: (0, 0))
    return pl.pallas_call(
        unpack_s_kernel,
        out_shape=[jax.ShapeDtypeStruct((frames, places, HEADS * HEAD_DIM), BF16)] * 4
        + [jax.ShapeDtypeStruct(halves[0].shape, F32)],
        grid=(HEADS // group,),
        in_specs=[pl.BlockSpec((frames, group, 4, places, HEAD_DIM), lambda i: (0, i, 0, 0, 0)), whole, whole],
        out_specs=[pl.BlockSpec((frames, places, group * HEAD_DIM), lambda i: (0, 0, i))] * 4 + [whole],
        compiler_params=params(16),
        cost_estimate=cost(0, 4 << 20),
        name="unpack_spatial",
    )(x.reshape(frames, HEADS, 4, places, HEAD_DIM), *halves)


def unpack_t_kernel(grads_ref, *refs):
    parts, outs, grads_out = refs[:8], refs[8:12], refs[12]
    half = outs[0].shape[-1] // 2
    part = half // 4
    grads_out[...] = grads_ref[...]
    row, x = lax.div(lax.axis_index("frame"), 4), lax.rem(lax.axis_index("frame"), 4)
    for j, ref in enumerate(parts):
        first = (1 - row if j >= 4 else row) * half + lax.rem(x + (0, *XSTEPS)[j % 4], 4) * part
        lanes = pl.ds(pl.multiple_of(first, part), part)
        for a, out in enumerate(outs):
            out[:, :, lanes] = ref[0, a]


def unpack_t(grads, parts):
    _, _, frames, places, part = parts[0].shape
    whole = pl.BlockSpec(grads.shape, lambda f: (0, 0))
    return pl.pallas_call(
        unpack_t_kernel,
        out_shape=[jax.ShapeDtypeStruct((frames, places, part * 8), BF16)] * 4
        + [jax.ShapeDtypeStruct(grads.shape, F32)],
        grid=(frames,),
        in_specs=[whole] + [pl.BlockSpec((1, 4, 1, places, part), lambda f: (0, 0, f, 0, 0))] * 8,
        out_specs=[pl.BlockSpec((1, places, part * 8), lambda f: (f, 0, 0))] * 4 + [whole],
        compiler_params=params(UNPACK_MIB),
        cost_estimate=cost(0, 4 << 20),
        name="unpack_temporal",
    )(grads, *parts)


def temporal_kernel(gains_ref, *refs):
    ins = [ref.at[0] for ref in refs[:8]]
    own, there, here, dgain_ref = refs[8], refs[9], refs[10:13], refs[13]
    there = [there.at[i] for i in range(4)]
    outs = [own.at[0]] + [ref.at[0] for ref in here] + there[1:] + there[:1]
    _, frames, places, width = ins[0].shape
    rows = 8 * frames * 16
    gain_q, gain_k = gains_ref[2:3, :], gains_ref[3:4, :]

    @pl.when(pl.program_id(0) == 0)
    def _():
        dgain_ref[...] = jnp.zeros_like(dgain_ref)

    row = lax.broadcasted_iota(jnp.int32, (rows, rows), 0)
    column = lax.broadcasted_iota(jnp.int32, (rows, rows), 1)
    same = (row % 16) == (column % 16)

    spots = [
        (slice(first, first + 16), slice(h, h + HEAD_DIM))
        for first in range(0, places, 16)
        for h in range(0, width, HEAD_DIM)
    ]
    for first in range(0, len(spots), TOGETHER):
        temporal_spots(spots[first : first + TOGETHER], ins, outs, dgain_ref, gain_q, gain_k, same)


def temporal_spots(spots, ins, outs, dgain_ref, gain_q, gain_k, same):
    frames = ins[0].shape[1]

    def take(a):
        return [jnp.concatenate([ref[a, f, *spot] for ref in ins for f in range(frames)], axis=0) for spot in spots]

    def each(f, *lists):
        return [f(*items) for items in zip(*lists)]

    def put(a, results):
        for spot, result in zip(spots, results):
            result = result.astype(BF16)
            for j, ref in enumerate(outs):
                for f in range(frames):
                    first = (j * frames + f) * 16
                    ref[a, f, *spot] = result[first : first + 16]

    def hat(x, gain):
        xf = x.astype(F32)
        return (xf * inverse_rms(xf) * gain).astype(BF16)

    query, key, value, dout = take(0), take(1), take(2), take(3)
    qh = each(lambda x: hat(x, gain_q), query)
    kh = each(lambda x: hat(x, gain_k), key)
    expo = each(lambda q, k: jnp.where(same, jnp.exp(dot(q, k, 1, 1) * SCALE), 0.0), qh, kh)
    probs = each(lambda e: e / jnp.sum(e, axis=-1, keepdims=True), expo)
    probs_b = each(lambda p: p.astype(BF16), probs)
    out = each(lambda p, v: dot(p, v, 1, 0), probs_b, value)
    dprob = each(lambda d, v: dot(d, v, 1, 1), dout, value)
    put(0, out)
    delta = each(lambda d, o: jnp.sum(d.astype(F32) * o, axis=-1, keepdims=True), dout, out)
    dscore = each(lambda p, dp, d: (p * (dp - d)).astype(BF16), probs, dprob, delta)
    put(3, each(lambda p, d: dot(p, d, 0, 0), probs_b, dout))
    dqh = each(lambda ds, k: dot(ds, k, 1, 0) * SCALE, dscore, kh)
    dkh = each(lambda ds, q: dot(ds, q, 0, 0) * SCALE, dscore, qh)
    for a, grads, given, gain in ((1, dqh, query, gain_q), (2, dkh, key, gain_k)):
        back = each(lambda g, x, gain=gain: norm_back(g, x, gain), grads, given)
        put(a, [dx for dx, _ in back])
        dgain_ref[a - 1 : a, :] += sum(dgain for _, dgain in back)


def temporal(gains, parts):
    _, arrays, frames, places, width = parts[0].shape
    sizes = (1, 4, 1, 1, 1)

    def block(n):
        return pl.BlockSpec((n, arrays, frames, TEMPORAL_ROWS, width), lambda i: (0, 0, 0, i, 0))

    res = pl.pallas_call(
        temporal_kernel,
        out_shape=[jax.ShapeDtypeStruct((n, arrays, frames, places, width), BF16) for n in sizes]
        + [jax.ShapeDtypeStruct((2, HEAD_DIM), F32)],
        grid=(places // TEMPORAL_ROWS,),
        in_specs=[pl.BlockSpec(gains.shape, lambda i: (0, 0))] + [block(1)] * 8,
        out_specs=[block(n) for n in sizes] + [pl.BlockSpec((2, HEAD_DIM), lambda i: (0, 0))],
        compiler_params=params(TEMPORAL_MIB),
        cost_estimate=cost(TEMPORAL_FLOPS, 4 << 20, 8 * 65536),
        name="temporal_attention",
    )(gains, *parts)
    return res[0], res[1], res[2:5], res[5]


def spatial_kernel(
    gains_ref, grads_t_ref, x_ref, home_ref, dgain_ref, qh, kh, kh_t, v_t, expo, dscore, out_t, dp_t, dp_n, dq_t, out_ref, sem
):
    tiles, _, places, depth = x_ref.shape
    seq = tiles * places
    per = BLOCK // places
    gain_q, gain_k = gains_ref[0:1, :], gains_ref[1:2, :]

    def rows_of(b):
        return pl.ds(pl.multiple_of(b * BLOCK, BLOCK), BLOCK)

    def read(a, b):
        return x_ref[pl.ds(b * per, per), a].reshape(BLOCK, depth)

    def write(a, b, value):
        out_ref[pl.ds(b * per, per), a] = value.astype(BF16).reshape(per, places, depth)

    def prepare(b, _):
        rows = rows_of(b)
        qf = read(0, b).astype(F32)
        qh[rows, :] = (qf * inverse_rms(qf) * gain_q).astype(BF16)
        kf = read(1, b).astype(F32)
        k_hat = (kf * inverse_rms(kf) * gain_k).astype(BF16)
        kh[rows, :] = k_hat
        kh_t[:, rows] = k_hat.T
        v_t[0:depth, rows] = read(2, b).T
        v_t[depth:, rows] = jnp.ones((ONES, BLOCK), BF16)
        return 0

    lax.fori_loop(0, seq // BLOCK, prepare, 0)

    def forward(b, _):
        rows = rows_of(b)
        q_b = qh[rows, :]
        for c in range(seq // BLOCK):
            keys = slice(c * BLOCK, (c + 1) * BLOCK)
            scores = dot(kh[keys, :], q_b, 1, 1)
            expo[keys, rows] = jnp.exp2(scores * (SCALE * LOG2E)).astype(BF16)
        out_t[...] = dot(v_t[...], expo[:, rows], 1, 0)
        inverse = 1.0 / out_t[depth : depth + 1, :]
        o_t = out_t[0:depth, :] * inverse
        write(0, b, o_t.astype(BF16).T)
        d_t = (read(3, b).T.astype(F32) * inverse).astype(BF16)
        delta = jnp.sum(d_t.astype(F32) * o_t, axis=0, keepdims=True)
        dp_t[:, rows] = d_t
        dp_n[rows, :] = d_t.T
        for c in range(seq // BLOCK):
            keys = slice(c * BLOCK, (c + 1) * BLOCK)
            value = x_ref[c * per : (c + 1) * per, 2].reshape(BLOCK, depth)
            grad = dot(value, d_t, 1, 0)
            dscore[keys, rows] = (expo[keys, rows].astype(F32) * (grad - delta)).astype(BF16)
        dq_t[...] = dot(kh_t[...], dscore[:, rows], 1, 0) * SCALE
        dquery, dgain = norm_back(dq_t[...].T, read(0, b), gain_q)
        write(1, b, dquery)
        dgain_ref[0:1, :] += dgain
        sending(b, 0).start()
        return 0

    def sending(b, phase):
        part = (pl.ds(b * per, per), pl.ds(2 * phase, 2))
        return pltpu.make_async_copy(out_ref.at[part], home_ref.at[part], sem.at[phase, b])

    dgain_ref[0:2, :] = jnp.zeros((2, depth), F32)
    dgain_ref[2:4, :] = grads_t_ref[...]
    lax.fori_loop(0, seq // BLOCK, forward, 0)

    def backward(b, _):
        rows = rows_of(b)
        dkh = dot(dscore[rows, :], qh[...], 1, 0) * SCALE
        dkey, dgain = norm_back(dkh, read(1, b), gain_k)
        write(2, b, dkey)
        dgain_ref[1:2, :] += dgain
        write(3, b, dot(expo[rows, :], dp_n[...], 1, 0))
        sending(b, 1).start()
        return 0

    lax.fori_loop(0, seq // BLOCK, backward, 0)
    for phase in range(2):
        for b in range(seq // BLOCK):
            sending(b, phase).wait()


def spatial(gains, grads_t, x):
    tiles, _, places, depth = x.shape
    seq = tiles * places
    whole = pl.BlockSpec(memory_space=pltpu.VMEM)
    return pl.pallas_call(
        spatial_kernel,
        out_shape=[jax.ShapeDtypeStruct(x.shape, BF16), jax.ShapeDtypeStruct((4, depth), F32)],
        in_specs=[whole, whole, whole],
        out_specs=[pl.BlockSpec(memory_space=pl.ANY), whole],
        scratch_shapes=[
            pltpu.VMEM((seq, depth), BF16),
            pltpu.VMEM((seq, depth), BF16),
            pltpu.VMEM((depth, seq), BF16),
            pltpu.VMEM((depth + ONES, seq), BF16),
            pltpu.VMEM((seq, seq), BF16),
            pltpu.VMEM((seq, seq), BF16),
            pltpu.VMEM((depth + ONES, BLOCK), F32),
            pltpu.VMEM((depth, seq), BF16),
            pltpu.VMEM((seq, depth), BF16),
            pltpu.VMEM((depth, BLOCK), F32),
            pltpu.VMEM(x.shape, BF16),
            pltpu.SemaphoreType.DMA((2, seq // BLOCK)),
        ],
        compiler_params=params(36),
        cost_estimate=cost(6 * 2 * seq * seq * depth, 4 << 20, seq * seq),
        name="spatial_attention",
    )(gains, grads_t, x)


def after_kernel(x_ref, *refs):
    pass


def after(x, others):
    anywhere = pl.BlockSpec(memory_space=pl.ANY)
    return pl.pallas_call(
        after_kernel,
        out_shape=jax.ShapeDtypeStruct(x.shape, x.dtype),
        in_specs=[anywhere] * (1 + len(others)),
        out_specs=anywhere,
        input_output_aliases={0: 0},
        compiler_params=params(1),
        cost_estimate=cost(0, 1024),
        name="after",
    )(x, *others)


def over_tile(x):
    count, arrays, places, depth = x.shape
    x = x.reshape(count, arrays * places, depth)
    return lax.all_to_all(x, "tile", split_axis=0, concat_axis=0, tiled=True).reshape(count, arrays, places, depth)


def along_x(x, step):
    return lax.ppermute(x, "frame", [(i, i // 4 * 4 + (i + step) % 4) for i in range(8)])


def across(x):
    return lax.ppermute(x, "frame", [(i, (i + 4) % 8) for i in range(8)])


def from_partner(x, axis, bit):
    size = 8 if axis == "frame" else 32
    return lax.ppermute(x, axis, [(i, i ^ bit) for i in range(size)])


def total_off_z(x):
    for axis, bit in (("frame", 1), ("frame", 2), ("frame", 4), ("tile", 1), ("tile", 2)):
        x = x + from_partner(x, axis, bit)
    return x


def total_z(x):
    got = []
    for near, far in ((None, 4), (1, 5), (2, 6), (3, 7)):
        perm = [(i, i ^ (4 * far)) for i in range(1, 32, 2)]
        if near is not None:
            perm += [(i, i ^ (4 * near)) for i in range(0, 32, 2)]
        got.append(lax.ppermute(x, "tile", perm))
    got[0] = jnp.where(lax.axis_index("tile") % 2 == 0, x, got[0])
    half = (got[0] + got[1]) + (got[2] + got[3])
    return half, from_partner(half, "tile", 1)


def local(query_s, key_s, value_s, grad_out_s, query_t, key_t, value_t, grad_out_t, gains):
    frames = query_s.shape[0]
    given_t = (query_t, key_t, value_t, grad_out_t)

    onward, sent = pack(given_t, (query_s, key_s, value_s, grad_out_s))
    onward = across(onward)
    items = over_tile(sent)
    *here, there = pack_here(given_t)
    here = [here[0]] + [along_x(part, step) for part, step in zip(here[1:], XSTEPS)]
    parts = here
    for i, step in enumerate(XSTEPS):
        parts.append(along_x(onward[i : i + 1], step))
    parts.append(across(there))

    own, there, here, grads_t = temporal(gains, parts)
    there = across(there)
    here = [along_x(part, -step) for part, step in zip(here, XSTEPS)]
    there_x = [along_x(there[i + 1 : i + 2], -step) for i, step in enumerate(XSTEPS)]

    res, grads = spatial(gains, grads_t, items)
    home = over_tile(after(res, [there, *here[:HERE_FIRST]]))
    *outs_t, grads = unpack_t(total_off_z(grads), [own, *here, there, *there_x])
    *outs_s, gain_grads = unpack_s(home, total_z(grads), frames)
    return (*outs_s, *outs_t, gain_grads)


def solution(mesh):
    split = P("frame", "tile", None)
    return jax.shard_map(
        local,
        mesh=mesh,
        in_specs=(split,) * 8 + (P(),),
        out_specs=(split,) * 8 + (P(),),
        check_vma=False,
    )
```

```python
import functools

import jax
import jax.numpy as jnp
from jax import lax
from jax.experimental import pallas as pl
from jax.experimental.pallas import tpu as pltpu
from jax.sharding import PartitionSpec as P

HEADS = 16
HEAD_DIM = 128
EPS = 1e-06
SCALE = HEAD_DIM**-0.5
LOG2E = 1.4426950408889634
BF16 = jnp.bfloat16
F32 = jnp.float32
SEQ = 2048
BLOCK = 1024
ONES = 16
TEMPORAL_FLOPS = 30 * 10**9
XSTEPS = (1, 3, 2)
TEMPORAL_MIB = 56
UNPACK_MIB = 24
TEMPORAL_ROWS = 32
TOGETHER = 4


def dot(a, b, ca, cb):
    return lax.dot_general(a, b, (((ca,), (cb,)), ((), ())), preferred_element_type=F32)


def params(mib):
    return pltpu.CompilerParams(vmem_limit_bytes=mib << 20)


def cost(flops, nbytes, trans=0):
    return pl.CostEstimate(flops=flops, bytes_accessed=nbytes, transcendentals=trans)


def inverse_rms(xf):
    return lax.rsqrt(jnp.mean(xf * xf, axis=-1, keepdims=True) + EPS)


def norm_back(grad_hat, x, gain):
    xf = x.astype(F32)
    inverse = inverse_rms(xf)
    unit = xf * inverse
    scaled = grad_hat * gain
    dgain = jnp.sum(grad_hat * unit, axis=0, keepdims=True)
    dx = inverse * (scaled - unit * jnp.mean(scaled * unit, axis=-1, keepdims=True))
    return dx.astype(BF16), dgain


def places_of_x(width):
    x = lax.rem(lax.axis_index("frame"), 4)
    return [pl.ds(pl.multiple_of(lax.rem(x + step, 4) * width, width), width) for step in (0, *XSTEPS)]


def row_lanes(other, width):
    row = lax.div(lax.axis_index("frame"), 4)
    row = 1 - row if other else row
    return pl.ds(pl.multiple_of(row * width, width), width)


def pack_kernel(*refs):
    far, near, there_ref, sent_ref = refs[:4], refs[4:8], refs[8], refs[9]
    far_in, near_in, there, sent, sem_far, sem_near, sem_there, sem_sent = refs[10:]
    frames, places, half = far_in.shape[1:]
    part = half // 4
    lanes = row_lanes(True, half)

    def fetch_far(a):
        return pltpu.make_async_copy(far[a].at[:, :, lanes], far_in.at[a], sem_far.at[a])

    def fetch_near(a, f):
        return pltpu.make_async_copy(near[a].at[f], near_in.at[a, f], sem_near.at[a, f])

    def send_there(a):
        return pltpu.make_async_copy(there.at[:, a], there_ref.at[:, a], sem_there.at[a])

    def send_sent(a, f):
        heads = pl.ds(f * HEADS, HEADS)
        return pltpu.make_async_copy(sent.at[heads, a], sent_ref.at[heads, a], sem_sent.at[a, f])

    for a in range(4):
        fetch_far(a).start()
    for a in range(4):
        for f in range(frames):
            fetch_near(a, f).start()
    spans = places_of_x(part)
    for a in range(4):
        fetch_far(a).wait()
        for i, span in enumerate(spans[1:]):
            there[i, a] = far_in[a, :, :, span]
        send_there(a).start()
    for a in range(4):
        for f in range(frames):
            fetch_near(a, f).wait()
            for h in range(HEADS):
                sent[f * HEADS + h, a] = near_in[a, f, :, h * HEAD_DIM : (h + 1) * HEAD_DIM]
            send_sent(a, f).start()
    for a in range(4):
        send_there(a).wait()
        for f in range(frames):
            send_sent(a, f).wait()


def pack(far, near):
    frames, places, width = near[0].shape
    there = (3, 4, frames, places, width // 8)
    sent = (frames * HEADS, 4, places, HEAD_DIM)
    anywhere = pl.BlockSpec(memory_space=pl.ANY)
    return pl.pallas_call(
        pack_kernel,
        out_shape=[jax.ShapeDtypeStruct(there, BF16)] + [jax.ShapeDtypeStruct(sent, BF16)],
        in_specs=[anywhere] * 8,
        out_specs=[anywhere] * 2,
        scratch_shapes=[
            pltpu.VMEM((4, frames, places, width // 2), BF16),
            pltpu.VMEM((4, frames, places, width), BF16),
            pltpu.VMEM(there, BF16),
            pltpu.VMEM(sent, BF16),
            pltpu.SemaphoreType.DMA((4,)),
            pltpu.SemaphoreType.DMA((4, frames)),
            pltpu.SemaphoreType.DMA((4,)),
            pltpu.SemaphoreType.DMA((4, frames)),
        ],
        compiler_params=params(60),
        cost_estimate=cost(0, 6 << 20),
        name="pack",
    )(*far, *near)


def pack_here_kernel(q_ref, k_ref, v_ref, d_ref, *refs):
    outs, far_out, held, sem, sem_far = refs[:4], refs[4], refs[5], refs[6], refs[7]
    lanes = row_lanes(False, held.shape[-1])
    part = held.shape[-1] // 4
    row, x = lax.div(lax.axis_index("frame"), 4), lax.rem(lax.axis_index("frame"), 4)
    far = pl.ds(pl.multiple_of(((1 - row) * 4 + x) * part, part), part)
    copies = [
        pltpu.make_async_copy(ref.at[:, :, lanes], held.at[a], sem.at[a])
        for a, ref in enumerate((q_ref, k_ref, v_ref, d_ref))
    ]
    far_copies = [
        pltpu.make_async_copy(ref.at[:, :, far], far_out.at[0, a], sem_far.at[a])
        for a, ref in enumerate((q_ref, k_ref, v_ref, d_ref))
    ]
    for copy in copies + far_copies:
        copy.start()
    spans = places_of_x(part)
    for a, copy in enumerate(copies):
        copy.wait()
        for out, span in zip(outs, spans):
            out[0, a] = held[a, :, :, span]
    for copy in far_copies:
        copy.wait()


def pack_here(arrays):
    frames, places, width = arrays[0].shape
    return pl.pallas_call(
        pack_here_kernel,
        out_shape=[jax.ShapeDtypeStruct((1, 4, frames, places, width // 8), BF16)] * 5,
        in_specs=[pl.BlockSpec(memory_space=pl.ANY)] * 4,
        out_specs=[pl.BlockSpec(memory_space=pltpu.VMEM)] * 5,
        scratch_shapes=[
            pltpu.VMEM((4, frames, places, width // 2), BF16),
            pltpu.SemaphoreType.DMA((4,)),
            pltpu.SemaphoreType.DMA((4,)),
        ],
        compiler_params=params(56),
        cost_estimate=cost(0, 2 << 20),
        name="pack_here",
    )(*arrays)


def unpack_s_kernel(x_ref, half_ref, other_ref, *out_refs):
    heads = x_ref.shape[1]
    out_refs[4][...] = half_ref[...] + other_ref[...]
    for a, ref in enumerate(out_refs[:4]):
        for f in range(2):
            for h in range(heads):
                ref[f, :, h * HEAD_DIM : (h + 1) * HEAD_DIM] = x_ref[f, h, a]


def unpack_s(x, halves, frames):
    places = x.shape[2]
    group = 4
    whole = pl.BlockSpec(halves[0].shape, lambda i: (0, 0))
    return pl.pallas_call(
        unpack_s_kernel,
        out_shape=[jax.ShapeDtypeStruct((frames, places, HEADS * HEAD_DIM), BF16)] * 4
        + [jax.ShapeDtypeStruct(halves[0].shape, F32)],
        grid=(HEADS // group,),
        in_specs=[pl.BlockSpec((frames, group, 4, places, HEAD_DIM), lambda i: (0, i, 0, 0, 0)), whole, whole],
        out_specs=[pl.BlockSpec((frames, places, group * HEAD_DIM), lambda i: (0, 0, i))] * 4 + [whole],
        compiler_params=params(16),
        cost_estimate=cost(0, 4 << 20),
        name="unpack_spatial",
    )(x.reshape(frames, HEADS, 4, places, HEAD_DIM), *halves)


def unpack_t_kernel(grads_ref, *refs):
    parts, outs, grads_out = refs[:8], refs[8:12], refs[12]
    half = outs[0].shape[-1] // 2
    part = half // 4
    grads_out[...] = grads_ref[...]
    row, x = lax.div(lax.axis_index("frame"), 4), lax.rem(lax.axis_index("frame"), 4)
    for j, ref in enumerate(parts):
        first = (1 - row if j >= 4 else row) * half + lax.rem(x + (0, *XSTEPS)[j % 4], 4) * part
        lanes = pl.ds(pl.multiple_of(first, part), part)
        for a, out in enumerate(outs):
            out[:, :, lanes] = ref[0, a]


def unpack_t(grads, parts):
    _, _, frames, places, part = parts[0].shape
    whole = pl.BlockSpec(grads.shape, lambda f: (0, 0))
    return pl.pallas_call(
        unpack_t_kernel,
        out_shape=[jax.ShapeDtypeStruct((frames, places, part * 8), BF16)] * 4
        + [jax.ShapeDtypeStruct(grads.shape, F32)],
        grid=(frames,),
        in_specs=[whole] + [pl.BlockSpec((1, 4, 1, places, part), lambda f: (0, 0, f, 0, 0))] * 8,
        out_specs=[pl.BlockSpec((1, places, part * 8), lambda f: (f, 0, 0))] * 4 + [whole],
        compiler_params=params(UNPACK_MIB),
        cost_estimate=cost(0, 4 << 20),
        name="unpack_temporal",
    )(grads, *parts)


def temporal_kernel(gains_ref, *refs):
    ins = [ref.at[0] for ref in refs[:8]]
    own, onward, here, there, dgain_ref = refs[8], refs[9], refs[10:13], refs[13], refs[14]
    outs = [own.at[0]] + [ref.at[0] for ref in here] + [onward.at[i] for i in range(3)] + [there.at[0]]
    _, frames, places, width = ins[0].shape
    rows = 8 * frames * 16
    gain_q, gain_k = gains_ref[2:3, :], gains_ref[3:4, :]

    @pl.when(pl.program_id(0) == 0)
    def _():
        dgain_ref[...] = jnp.zeros_like(dgain_ref)

    row = lax.broadcasted_iota(jnp.int32, (rows, rows), 0)
    column = lax.broadcasted_iota(jnp.int32, (rows, rows), 1)
    same = (row % 16) == (column % 16)

    spots = [
        (slice(first, first + 16), slice(h, h + HEAD_DIM))
        for first in range(0, places, 16)
        for h in range(0, width, HEAD_DIM)
    ]
    for first in range(0, len(spots), TOGETHER):
        temporal_spots(spots[first : first + TOGETHER], ins, outs, dgain_ref, gain_q, gain_k, same)


def temporal_spots(spots, ins, outs, dgain_ref, gain_q, gain_k, same):
    frames = ins[0].shape[1]

    def take(a):
        return [jnp.concatenate([ref[a, f, *spot] for ref in ins for f in range(frames)], axis=0) for spot in spots]

    def each(f, *lists):
        return [f(*items) for items in zip(*lists)]

    def put(a, results):
        for spot, result in zip(spots, results):
            result = result.astype(BF16)
            for j, ref in enumerate(outs):
                for f in range(frames):
                    first = (j * frames + f) * 16
                    ref[a, f, *spot] = result[first : first + 16]

    def hat(x, gain):
        xf = x.astype(F32)
        return (xf * inverse_rms(xf) * gain).astype(BF16)

    query, key, value, dout = take(0), take(1), take(2), take(3)
    qh = each(lambda x: hat(x, gain_q), query)
    kh = each(lambda x: hat(x, gain_k), key)
    expo = each(lambda q, k: jnp.where(same, jnp.exp(dot(q, k, 1, 1) * SCALE), 0.0), qh, kh)
    probs = each(lambda e: e / jnp.sum(e, axis=-1, keepdims=True), expo)
    probs_b = each(lambda p: p.astype(BF16), probs)
    out = each(lambda p, v: dot(p, v, 1, 0), probs_b, value)
    dprob = each(lambda d, v: dot(d, v, 1, 1), dout, value)
    put(0, out)
    delta = each(lambda d, o: jnp.sum(d.astype(F32) * o, axis=-1, keepdims=True), dout, out)
    dscore = each(lambda p, dp, d: (p * (dp - d)).astype(BF16), probs, dprob, delta)
    put(3, each(lambda p, d: dot(p, d, 0, 0), probs_b, dout))
    dqh = each(lambda ds, k: dot(ds, k, 1, 0) * SCALE, dscore, kh)
    dkh = each(lambda ds, q: dot(ds, q, 0, 0) * SCALE, dscore, qh)
    for a, grads, given, gain in ((1, dqh, query, gain_q), (2, dkh, key, gain_k)):
        back = each(lambda g, x, gain=gain: norm_back(g, x, gain), grads, given)
        put(a, [dx for dx, _ in back])
        dgain_ref[a - 1 : a, :] += sum(dgain for _, dgain in back)


def temporal(gains, parts):
    _, arrays, frames, places, width = parts[0].shape
    sizes = (1, 3, 1, 1, 1, 1)

    def block(n):
        return pl.BlockSpec((n, arrays, frames, TEMPORAL_ROWS, width), lambda i: (0, 0, 0, i, 0))

    res = pl.pallas_call(
        temporal_kernel,
        out_shape=[jax.ShapeDtypeStruct((n, arrays, frames, places, width), BF16) for n in sizes]
        + [jax.ShapeDtypeStruct((2, HEAD_DIM), F32)],
        grid=(places // TEMPORAL_ROWS,),
        in_specs=[pl.BlockSpec(gains.shape, lambda i: (0, 0))] + [block(1)] * 8,
        out_specs=[block(n) for n in sizes] + [pl.BlockSpec((2, HEAD_DIM), lambda i: (0, 0))],
        compiler_params=params(TEMPORAL_MIB),
        cost_estimate=cost(TEMPORAL_FLOPS, 4 << 20, 8 * 65536),
        name="temporal_attention",
    )(gains, *parts)
    return res[0], res[1], res[2:5], res[5], res[6]


def spatial_kernel(
    gains_ref, grads_t_ref, x_ref, home_ref, dgain_ref, qh, kh, kh_t, v_t, expo, dscore, out_t, dp_t, dp_n, dq_t, out_ref, sem
):
    tiles, _, places, depth = x_ref.shape
    seq = tiles * places
    per = BLOCK // places
    gain_q, gain_k = gains_ref[0:1, :], gains_ref[1:2, :]

    def rows_of(b):
        return pl.ds(pl.multiple_of(b * BLOCK, BLOCK), BLOCK)

    def read(a, b):
        return x_ref[pl.ds(b * per, per), a].reshape(BLOCK, depth)

    def write(a, b, value):
        out_ref[pl.ds(b * per, per), a] = value.astype(BF16).reshape(per, places, depth)

    def prepare(b, _):
        rows = rows_of(b)
        qf = read(0, b).astype(F32)
        qh[rows, :] = (qf * inverse_rms(qf) * gain_q).astype(BF16)
        kf = read(1, b).astype(F32)
        k_hat = (kf * inverse_rms(kf) * gain_k).astype(BF16)
        kh[rows, :] = k_hat
        kh_t[:, rows] = k_hat.T
        v_t[0:depth, rows] = read(2, b).T
        v_t[depth:, rows] = jnp.ones((ONES, BLOCK), BF16)
        return 0

    lax.fori_loop(0, seq // BLOCK, prepare, 0)

    def forward(b, _):
        rows = rows_of(b)
        q_b = qh[rows, :]
        for c in range(seq // BLOCK):
            keys = slice(c * BLOCK, (c + 1) * BLOCK)
            scores = dot(kh[keys, :], q_b, 1, 1)
            expo[keys, rows] = jnp.exp2(scores * (SCALE * LOG2E)).astype(BF16)
        out_t[...] = dot(v_t[...], expo[:, rows], 1, 0)
        inverse = 1.0 / out_t[depth : depth + 1, :]
        o_t = out_t[0:depth, :] * inverse
        write(0, b, o_t.astype(BF16).T)
        d_t = (read(3, b).T.astype(F32) * inverse).astype(BF16)
        delta = jnp.sum(d_t.astype(F32) * o_t, axis=0, keepdims=True)
        dp_t[:, rows] = d_t
        dp_n[rows, :] = d_t.T
        for c in range(seq // BLOCK):
            keys = slice(c * BLOCK, (c + 1) * BLOCK)
            value = x_ref[c * per : (c + 1) * per, 2].reshape(BLOCK, depth)
            grad = dot(value, d_t, 1, 0)
            dscore[keys, rows] = (expo[keys, rows].astype(F32) * (grad - delta)).astype(BF16)
        dq_t[...] = dot(kh_t[...], dscore[:, rows], 1, 0) * SCALE
        dquery, dgain = norm_back(dq_t[...].T, read(0, b), gain_q)
        write(1, b, dquery)
        dgain_ref[0:1, :] += dgain
        sending(b, 0).start()
        return 0

    def sending(b, phase):
        part = (pl.ds(b * per, per), pl.ds(2 * phase, 2))
        return pltpu.make_async_copy(out_ref.at[part], home_ref.at[part], sem.at[phase, b])

    dgain_ref[0:2, :] = jnp.zeros((2, depth), F32)
    dgain_ref[2:4, :] = grads_t_ref[...]
    lax.fori_loop(0, seq // BLOCK, forward, 0)

    def backward(b, _):
        rows = rows_of(b)
        dkh = dot(dscore[rows, :], qh[...], 1, 0) * SCALE
        dkey, dgain = norm_back(dkh, read(1, b), gain_k)
        write(2, b, dkey)
        dgain_ref[1:2, :] += dgain
        write(3, b, dot(expo[rows, :], dp_n[...], 1, 0))
        sending(b, 1).start()
        return 0

    lax.fori_loop(0, seq // BLOCK, backward, 0)
    for phase in range(2):
        for b in range(seq // BLOCK):
            sending(b, phase).wait()


def spatial(gains, grads_t, x):
    tiles, _, places, depth = x.shape
    seq = tiles * places
    whole = pl.BlockSpec(memory_space=pltpu.VMEM)
    return pl.pallas_call(
        spatial_kernel,
        out_shape=[jax.ShapeDtypeStruct(x.shape, BF16), jax.ShapeDtypeStruct((4, depth), F32)],
        in_specs=[whole, whole, whole],
        out_specs=[pl.BlockSpec(memory_space=pl.ANY), whole],
        scratch_shapes=[
            pltpu.VMEM((seq, depth), BF16),
            pltpu.VMEM((seq, depth), BF16),
            pltpu.VMEM((depth, seq), BF16),
            pltpu.VMEM((depth + ONES, seq), BF16),
            pltpu.VMEM((seq, seq), BF16),
            pltpu.VMEM((seq, seq), BF16),
            pltpu.VMEM((depth + ONES, BLOCK), F32),
            pltpu.VMEM((depth, seq), BF16),
            pltpu.VMEM((seq, depth), BF16),
            pltpu.VMEM((depth, BLOCK), F32),
            pltpu.VMEM(x.shape, BF16),
            pltpu.SemaphoreType.DMA((2, seq // BLOCK)),
        ],
        compiler_params=params(36),
        cost_estimate=cost(6 * 2 * seq * seq * depth, 4 << 20, seq * seq),
        name="spatial_attention",
    )(gains, grads_t, x)


def after_kernel(x_ref, *refs):
    pass


def after(x, others):
    anywhere = pl.BlockSpec(memory_space=pl.ANY)
    return pl.pallas_call(
        after_kernel,
        out_shape=jax.ShapeDtypeStruct(x.shape, x.dtype),
        in_specs=[anywhere] * (1 + len(others)),
        out_specs=anywhere,
        input_output_aliases={0: 0},
        compiler_params=params(1),
        cost_estimate=cost(0, 1024),
        name="after",
    )(x, *others)


def over_tile(x):
    count, arrays, places, depth = x.shape
    x = x.reshape(count, arrays * places, depth)
    return lax.all_to_all(x, "tile", split_axis=0, concat_axis=0, tiled=True).reshape(count, arrays, places, depth)


def along_x(x, step):
    return lax.ppermute(x, "frame", [(i, i // 4 * 4 + (i + step) % 4) for i in range(8)])


def across(x):
    return lax.ppermute(x, "frame", [(i, (i + 4) % 8) for i in range(8)])


def from_partner(x, axis, bit):
    size = 8 if axis == "frame" else 32
    return lax.ppermute(x, axis, [(i, i ^ bit) for i in range(size)])


def total_off_z(x):
    for axis, bit in (("frame", 1), ("frame", 2), ("frame", 4), ("tile", 1), ("tile", 2)):
        x = x + from_partner(x, axis, bit)
    return x


def total_z(x):
    got = []
    for near, far in ((None, 4), (1, 5), (2, 6), (3, 7)):
        perm = [(i, i ^ (4 * far)) for i in range(1, 32, 2)]
        if near is not None:
            perm += [(i, i ^ (4 * near)) for i in range(0, 32, 2)]
        got.append(lax.ppermute(x, "tile", perm))
    got[0] = jnp.where(lax.axis_index("tile") % 2 == 0, x, got[0])
    half = (got[0] + got[1]) + (got[2] + got[3])
    return half, from_partner(half, "tile", 1)


def local(query_s, key_s, value_s, grad_out_s, query_t, key_t, value_t, grad_out_t, gains):
    frames = query_s.shape[0]
    given_t = (query_t, key_t, value_t, grad_out_t)

    onward, sent = pack(given_t, (query_s, key_s, value_s, grad_out_s))
    onward = across(onward)
    items = over_tile(sent)
    *here, there = pack_here(given_t)
    here = [here[0]] + [along_x(part, step) for part, step in zip(here[1:], XSTEPS)]
    parts = here
    for i, step in enumerate(XSTEPS):
        parts.append(along_x(onward[i : i + 1], step))
    parts.append(across(there))

    own, onward, here, there, grads_t = temporal(gains, parts)
    onward, there = across(onward), across(there)
    here = [along_x(part, -step) for part, step in zip(here, XSTEPS)]
    onward_x = [along_x(onward[i : i + 1], -step) for i, step in enumerate(XSTEPS)]

    res, grads = spatial(gains, grads_t, items)
    home = over_tile(after(res, [onward, *here]))
    *outs_t, grads = unpack_t(total_off_z(grads), [own, *here, there, *onward_x])
    *outs_s, gain_grads = unpack_s(home, total_z(grads), frames)
    return (*outs_s, *outs_t, gain_grads)


def solution(mesh):
    split = P("frame", "tile", None)
    return jax.shard_map(
        local,
        mesh=mesh,
        in_specs=(split,) * 8 + (P(),),
        out_specs=(split,) * 8 + (P(),),
        check_vma=False,
    )
```
